256 devices in a mesh: orb: 32 (over x, y, core), grid: 8 (over z).
Axes of the slice: x: 4, y: 4, z: 8, core: 2. Of those that a mesh axis runs over, the one named last changes fastest.
Arguments:
- orbitals: bfloat16 [256, 64, 4096], P('orb', 'grid'), may hold values from -6 to 10
- pair_list: int32 [2, 512], P(None, 'orb'), may hold values from -1 to 255, as said below
- box_anchor: int32 [2, 256], replicated, may hold values from 0 to 16
Outputs:
- potentials: bfloat16 [256, 64, 4096], P('orb', 'grid')
- energies: float32 [256], P('orb')
The draws below stay inside these ranges and needn't reach their ends.
Inputs may be any that keep to these rules, and one draw needn't show every extreme that they name: `pair_list`: columns 16 * d to 16 * (d + 1) - 1 belong to index d of orb: row 0 names an orbital of that index (8 * d to 8 * (d + 1) - 1), row 1 an orbital of another index or -1 for an empty entry. Empty entries stand at the end of an index's columns; every index has at least 12 live entries and some index none empty. At most 2 live entries of one index name orbitals of one other index, and every index has, for at least one other index, exactly 2 live entries naming its orbitals.
All inputs are finite; a program needn't handle non-finite values.
Results may differ from the reference program's by a relative error of at most 0.0047.
Values may be sent and summed in bfloat16 or wider, within the bound.
No kernel may reach another device: no remote copies, remote signals or barrier semaphores. Data moves between devices by JAX's collectives and lax.ppermute only.
A program may use at most 192 MiB of HBM per device.

```python
import jax
import jax.numpy as jnp
from jax import lax

BOX = 64
ORB_DEV = 8
PAIRS_DEV = 16
SHIFT = 16
SLOTS = 2
ORBITALS = 256
PAIRS = 512
N_ORB = 32


def draw_orbitals(key, part):
    key = jax.random.fold_in(key, 5)
    key_core, key_scale = jax.random.split(key)
    shape_all = (ORBITALS, BOX, BOX * BOX)
    scale = jnp.exp2(2.0 * jax.random.uniform(key_scale, shape_all, jnp.float32, -1.0, 1.0))
    core = 0.4 + 0.6 * jax.random.normal(key_core, shape_all, jnp.float32)
    core = jnp.clip(core, -1.5, 2.5)
    return (scale * core).astype(jnp.bfloat16)


def draw_pair_list(key, part):
    key = jax.random.fold_in(key, 9)
    key_full, key_live, key_rest = jax.random.split(key, 3)
    full_device = jax.random.randint(key_full, (), 0, N_ORB)
    devices = jnp.arange(N_ORB)
    live_count = jax.random.randint(key_live, (N_ORB,), 3 * PAIRS_DEV // 4, PAIRS_DEV + 1)
    live_count = jnp.where(devices == full_device, PAIRS_DEV, live_count)
    device_keys = jax.random.split(key_rest, N_ORB)

    def one_device(device_key, source, live_here):
        key_order, key_mate, key_owner = jax.random.split(device_key, 3)
        shuffled = jax.random.permutation(key_order, (N_ORB - 2) * SLOTS)[:PAIRS_DEV - SLOTS]
        far_dest = (source + 2 + shuffled // SLOTS) % N_ORB
        near_dest = jnp.full((SLOTS,), (source + 1) % N_ORB)
        target_dev = jnp.concatenate([near_dest, far_dest])
        partner = target_dev * ORB_DEV + jax.random.randint(key_mate, (PAIRS_DEV,), 0, ORB_DEV)
        owner_id = source * ORB_DEV + jax.random.randint(key_owner, (PAIRS_DEV,), 0, ORB_DEV)
        partner = jnp.where(jnp.arange(PAIRS_DEV) < live_here, partner, -1)
        return jnp.stack([owner_id, partner])
    listed = jax.vmap(one_device)(device_keys, devices, live_count)
    return jnp.transpose(listed, (1, 0, 2)).reshape(2, PAIRS).astype(jnp.int32)


def touch_ends(drawn, rng, least, largest):
    spot = [jax.random.randint(jax.random.fold_in(rng, axis), (), 0, length) for axis, length in enumerate(drawn.shape)]
    main_axis = drawn.shape.index(max(drawn.shape))
    next_to = spot[:main_axis] + [(spot[main_axis] + 1) % drawn.shape[main_axis]] + spot[main_axis + 1:]
    return drawn.at[tuple(spot)].set(least).at[tuple(next_to)].set(largest)


def setup_inputs(seed: int = 0) -> dict:
    arg_keys = jax.random.split(jax.random.key(seed), 4)
    return {
        "orbitals": draw_orbitals(jax.random.fold_in(arg_keys[3], 71), 0),
        "pair_list": draw_pair_list(jax.random.fold_in(arg_keys[3], 71), 0),
        "box_anchor": touch_ends(jax.random.randint(arg_keys[2], (2, ORBITALS), 0, SHIFT + 1), jax.random.fold_in(arg_keys[2], 1), 0, SHIFT).astype(jnp.int32),
    }


MU2 = 0.02

def sine_table(length):
    steps = jnp.arange(1, length + 1).astype(jnp.float32)
    angles = jnp.pi * steps[:, None] * steps[None, :] / (length + 1)
    return jnp.sqrt(2.0 / (length + 1)) * jnp.sin(angles)

def kernel_weights(length):
    steps = jnp.arange(1, length + 1).astype(jnp.float32)
    eigen_vals = 2.0 - 2.0 * jnp.cos(jnp.pi * steps / (length + 1))
    summed = eigen_vals[:, None, None] + eigen_vals[None, :, None] + eigen_vals[None, None, :]
    return MU2 / (summed + MU2)

def solve_box(density, sine_mat, weights):
    high = lax.Precision.HIGHEST
    coeffs = jnp.einsum('zxy,yk->zxk', density, sine_mat, precision=high)
    coeffs = jnp.einsum('zxk,xj->zjk', coeffs, sine_mat, precision=high)
    coeffs = lax.optimization_barrier(coeffs.astype(jnp.bfloat16)).astype(jnp.float32)
    coeffs = jnp.einsum('zjk,zi->ijk', coeffs, sine_mat, precision=high) * weights
    coeffs = jnp.einsum('ijk,iz->zjk', coeffs, sine_mat, precision=high)
    coeffs = lax.optimization_barrier(coeffs.astype(jnp.bfloat16)).astype(jnp.float32)
    coeffs = jnp.einsum('zjk,jx->zxk', coeffs, sine_mat, precision=high)
    return jnp.einsum('zxk,ky->zxy', coeffs, sine_mat, precision=high)

def shift_box(field_in, step_x, step_y):
    margin = SHIFT
    padded = jnp.pad(field_in, ((0, 0), (margin, margin), (margin, margin)))
    anchor = jnp.zeros((), jnp.int32)
    starts = (anchor, (margin + step_x).astype(jnp.int32), (margin + step_y).astype(jnp.int32))
    return lax.dynamic_slice(padded, starts, (field_in.shape[0], BOX, BOX))

def reference(orbitals, pair_list, box_anchor):
    sine_mat = sine_table(BOX)
    weights = kernel_weights(BOX)
    all_boxes = orbitals.reshape(ORBITALS, BOX, BOX, BOX)

    def self_term(orbital_box):
        wide_box = orbital_box.astype(jnp.float32)
        return wide_box * solve_box(wide_box * wide_box, sine_mat, weights)
    summed = lax.map(self_term, all_boxes)

    def pair_step(summed, pair_row):
        owner_id = pair_row[0]
        is_live = pair_row[1] >= 0
        mate_id = jnp.maximum(pair_row[1], 0)
        owner_box = lax.dynamic_index_in_dim(all_boxes, owner_id, 0, keepdims=False).astype(jnp.float32)
        mate_box = lax.dynamic_index_in_dim(all_boxes, mate_id, 0, keepdims=False).astype(jnp.float32)
        offset_xy = box_anchor[:, owner_id] - box_anchor[:, mate_id]
        moved_box = shift_box(mate_box, offset_xy[0], offset_xy[1])
        potential = solve_box(owner_box * moved_box, sine_mat, weights)
        own_term = jnp.where(is_live, moved_box * potential, 0.0)
        back_term = shift_box(owner_box * potential, -offset_xy[0], -offset_xy[1])
        back_term = lax.optimization_barrier(back_term.astype(jnp.bfloat16)).astype(jnp.float32)
        back_term = jnp.where(is_live, back_term, 0.0)
        summed = summed.at[owner_id].add(own_term)
        summed = summed.at[mate_id].add(back_term)
        return (summed, None)
    summed, unused = lax.scan(pair_step, summed, jnp.transpose(pair_list))
    energies = lax.optimization_barrier(jnp.sum(all_boxes.astype(jnp.float32) * summed, axis=(1, 2, 3)))
    potentials = summed.astype(jnp.bfloat16).reshape(ORBITALS, BOX, BOX * BOX)
    return (potentials, energies)
```

```python
import functools

import jax
import jax.numpy as jnp
import ml_dtypes
import numpy as np
from jax import lax
from jax.experimental import pallas as pl
from jax.experimental.pallas import tpu as pltpu
from jax.sharding import PartitionSpec as P

BOX = 64
LANES = 128
TILES = BOX * BOX // LANES
PLANES = 8
ROWS = TILES * PLANES
GRID = 8
PAIRS = GRID // 2
COMBOS = [(p, q) for q in range(PAIRS) for p in range(q)]
UP, DOWN, MIDDLE, CARRY, PAST_UP, PAST_DOWN, INSIDE, ACROSS = 0, 8, 16, 24, 27, 28, 29, 30
CHUNK = 8
ORB_DEV = 8
PAD = 10
MU2 = 0.02
BF16 = jnp.bfloat16
F32 = jnp.float32
VMEM_LIMIT = 40 * 1024 * 1024


def sine64():
    steps = np.arange(1, BOX + 1, dtype=np.float64)
    return np.sqrt(2.0 / (BOX + 1)) * np.sin(np.pi * steps[:, None] * steps[None, :] / (BOX + 1))


def high_low(table):
    high = table.astype(np.float32).astype(ml_dtypes.bfloat16)
    rest = table - high.astype(np.float64)
    return high, rest.astype(np.float32).astype(ml_dtypes.bfloat16)


def sine_factors():
    sine = sine64()
    zero = np.zeros((BOX, BOX))
    high, low = high_low(np.block([[sine, zero], [zero, sine]]))
    y_right = np.concatenate(
        [np.concatenate([high, low], 1), np.concatenate([high, np.zeros_like(high)], 1)], 0
    )
    half = 2 * np.arange(TILES)
    rows = []
    for h in range(2):
        rows.append(np.concatenate([sine[np.ix_(half + h, half + h)], sine[np.ix_(half + h, half + 1 - h)]], 1))
    high, low = high_low(np.concatenate(rows, 0))
    return jnp.asarray(y_right), jnp.asarray(np.concatenate([high, high, low], 1))


def z_factors(grid_index):
    steps = jnp.arange(1, BOX + 1).astype(F32)
    eigen = 2.0 - 2.0 * jnp.cos(jnp.pi * steps / (BOX + 1))
    s = (eigen[:, None] + eigen[None, :] + MU2).reshape(TILES, LANES)[None]
    theta = jnp.log(1.0 + 0.5 * s + jnp.sqrt(s + 0.25 * s * s))

    def number(n):
        return jnp.asarray(n).reshape(-1).astype(F32)[:, None, None]

    def rest(n):
        return 1.0 - jnp.exp(-2.0 * theta * number(n))

    def fall(n):
        return jnp.exp(-theta * number(n))

    z = grid_index * PLANES + jnp.arange(PLANES)
    up = fall(1) * rest(z) / rest(z + 1)
    down = fall(1) * rest(63 - z) / rest(64 - z)
    scale = MU2 / (rest(1) * rest(65))
    middle = scale * fall(1) * rest(z + 1) * rest(64 - z)
    pair = grid_index // 2
    e = jnp.arange(1, PAIRS)
    other = (pair - e) % PAIRS
    below = e <= pair
    away = jnp.where(below, 8 * grid_index - 16 * other - 16, 16 * other - 8 * grid_index - 8)
    first = jnp.where(below, 16 * other + 16, 64 - 16 * other)
    last = jnp.where(below, 8 * grid_index, 56 - 8 * grid_index)
    carry = fall(away) * rest(first) / rest(last)
    edge = 16 * pair + 8
    past_up = fall(8) * rest(edge) / rest(edge + 8)
    past_down = fall(8) * rest(64 - edge) / rest(72 - edge)
    inside = scale * fall(2) * rest(edge) * rest(64 - edge)
    m1 = jnp.stack([(pair - p) % PAIRS for p, _ in COMBOS])
    m2 = jnp.stack([(pair - q) % PAIRS for _, q in COMBOS])
    low, high = jnp.minimum(m1, m2), jnp.maximum(m1, m2)
    across = scale * fall(16 * (high - low) - 14) * rest(16 * low + 16) * rest(64 - 16 * high)
    return jnp.concatenate([up, down, middle, carry, past_up, past_down, inside, across], 0)


def lane_iota(rows):
    return lax.broadcasted_iota(jnp.int32, (rows, LANES), 1)


def split(value):
    high = value.astype(BF16)
    return high, (value - high.astype(F32)).astype(BF16)


def dot(left, right):
    return jnp.dot(left, right, preferred_element_type=F32)


def times_y(value, y_right):
    high, low = split(value)
    both = dot(jnp.concatenate([high, low], axis=1), y_right)
    return both[:, :LANES] + both[:, LANES:]


def times_x(planes, x_left):
    value = jnp.concatenate(planes, axis=1)
    other = jnp.concatenate([pltpu.roll(p, BOX, 1) for p in planes], axis=1)
    high, low = split(jnp.concatenate([value, other], axis=0))
    both = dot(x_left, jnp.concatenate([high, low, high], axis=0))
    first = lane_iota(TILES) < BOX
    out = []
    for z in range(PLANES):
        tile = both[:, LANES * z : LANES * (z + 1)]
        out.append(jnp.where(first, tile[:TILES], tile[TILES:]))
    return out


def shifted(value, step_x, step_y, buffer):
    buffer[PAD * 8 : PAD * 8 + ROWS, :] = value
    flat = step_x * BOX + step_y
    tiles = flat >> 7
    lanes = flat & 127
    start = pl.multiple_of((tiles + PAD) * 8, 8)
    window = buffer[pl.ds(start, ROWS + 8), :]
    window = pltpu.roll(window, (LANES - lanes) & 127, 1)
    lane = lane_iota(ROWS)
    moved = jnp.where(lane < LANES - lanes, window[:ROWS], window[8:])
    y_new = (lane & (BOX - 1)) + step_y
    return jnp.where((y_new >= 0) & (y_new < BOX), moved, 0.0)


def clear_margins(buffer):
    zero = jnp.zeros((PAD * 8, LANES), F32)
    buffer[: PAD * 8, :] = zero
    buffer[PAD * 8 + ROWS :, :] = zero


def column_sums(value):
    return jnp.sum(value, axis=0, keepdims=True)


def forward(rho, tables, held, coeffs, ends, message, energy, n):
    y_right, x_left, z_table = tables
    held[...] = times_y(rho, y_right[...])
    planes = times_x([held[pl.ds(z, TILES, stride=PLANES), :] for z in range(PLANES)], x_left[...])
    for z in range(PLANES):
        coeffs[n, TILES * z : TILES * (z + 1), :] = planes[z]
    above = jnp.zeros((TILES, LANES), F32)
    product = jnp.zeros((TILES, LANES), F32)
    for z in range(PLANES):
        above = z_table[UP + z] * above + planes[z]
        if energy is not None:
            product += z_table[MIDDLE + z] * planes[z] * (2.0 * above - planes[z])
    below = planes[PLANES - 1]
    for z in range(PLANES - 2, -1, -1):
        below = z_table[DOWN + z] * below + planes[z]
    both = jnp.concatenate([above, below], axis=0)
    ends[n] = both
    message[n] = both.astype(BF16)
    if energy is not None:
        energy[n : n + 1, :] = column_sums(product)


def pack_energy(energy, message):
    high = energy.astype(BF16).astype(F32)
    message[CHUNK, :16, :] = jnp.concatenate([high, energy - high], axis=0).astype(BF16)
    message[CHUNK, 16:, :] = jnp.zeros((2 * TILES - 16, LANES), BF16)


def unpack_energy(message):
    both = message[CHUNK, :16, :].astype(F32)
    return both[:8] + both[8:]


def halves(message, n):
    both = message[n].astype(F32)
    return both[:TILES], both[TILES:]


def between_pairs(pair, ends, z_table):
    product = jnp.zeros((TILES, LANES), F32)
    for i, (p, q) in enumerate(COMBOS):
        p_low = ((pair - p) & (PAIRS - 1)) < ((pair - q) & (PAIRS - 1))
        low = jnp.where(p_low, ends[p][0], ends[q][0])
        high = jnp.where(p_low, ends[q][1], ends[p][1])
        product += z_table[ACROSS + i] * low * high
    return 2.0 * column_sums(product)


def inverse(grid, near, sums, coeffs, tables, held, n):
    y_right, x_left, z_table = tables
    near_up, near_down = halves(near, n)
    upper = (grid & 1) == 1
    from_below = jnp.where(upper, near_up, 0.0)
    from_above = jnp.where(upper, 0.0, near_down)
    for e in range(1, PAIRS):
        below = e <= (grid >> 1)
        term = z_table[CARRY + e - 1] * sums[e - 1]
        from_below += jnp.where(below, term, 0.0)
        from_above += jnp.where(below, 0.0, term)
    planes = [coeffs[n, TILES * z : TILES * (z + 1), :] for z in range(PLANES)]
    ups = []
    for z in range(PLANES):
        from_below = z_table[UP + z] * from_below + planes[z]
        ups.append(from_below)
    solved = [None] * PLANES
    for z in range(PLANES - 1, -1, -1):
        carried = z_table[DOWN + z] * from_above
        solved[z] = z_table[MIDDLE + z] * (ups[z] + carried)
        from_above = planes[z] + carried
    full = times_y(jnp.concatenate(times_x(solved, x_left[...]), axis=0), y_right[...])
    for z in range(PLANES):
        held[pl.ds(z, TILES, stride=PLANES), :] = full[TILES * z : TILES * (z + 1)]
    return held[...]


def pair_scalars(perm, pairs, anchor, n):
    entry = perm[n]
    safe = jnp.maximum(entry, 0)
    owner = pairs[0, safe]
    mate = jnp.maximum(pairs[1, safe], 0)
    step_x = anchor[0, owner] - anchor[0, mate]
    step_y = anchor[1, owner] - anchor[1, mate]
    return entry >= 0, owner & (ORB_DEV - 1), mate >> 3, step_x, step_y


def plan_kernel(pairs, ask, perm, count):
    devices = ask.shape[0]
    entries = 2 * CHUNK
    for t in range(devices + 1):
        count[t] = 0
    for p in range(entries):
        perm[p] = -1
    mates = [pairs[1, p] for p in range(entries)]
    targets = [jnp.where(m >= 0, m >> 3, devices) for m in mates]
    for t in targets:
        count[t] = count[t] + 1
    spots = []
    used = [jnp.int32(0), jnp.int32(0)]
    for p in range(entries):
        seen = count[targets[p]]
        live = mates[p] >= 0
        first, second = live & (seen == 2), live & (seen == 3)
        count[targets[p]] = jnp.where(first, 3, seen)
        spots.append(jnp.where(first, used[0], jnp.where(second, CHUNK + used[1], -1)))
        used[0] += first.astype(jnp.int32)
        used[1] += second.astype(jnp.int32)
    row = lax.broadcasted_iota(jnp.int32, (devices, LANES), 0)
    lane = lax.broadcasted_iota(jnp.int32, (devices, LANES), 1)
    asks = jnp.full((devices, LANES), -1, jnp.int32)
    for p in range(entries):
        live = mates[p] >= 0
        single = live & (spots[p] < 0)
        early = single & (used[0] < CHUNK)
        late = single & (used[0] >= CHUNK)
        spot = jnp.where(early, used[0], jnp.where(late, CHUNK + used[1], spots[p]))
        used[0] += early.astype(jnp.int32)
        used[1] += late.astype(jnp.int32)

        @pl.when(live)
        def _():
            perm[spot] = p

        chunk = jnp.where(spot >= CHUNK, 1, 0)
        here = (row == jnp.where(live, targets[p], -1)) & (lane == chunk)
        asks = jnp.where(here, mates[p] & (ORB_DEV - 1), asks)
    ask[:, 0, :] = asks


def rows_kernel(orb, orb_rows):
    for n in range(ORB_DEV):
        wide = orb[n].astype(F32)
        box = jnp.concatenate([wide[:, LANES * t : LANES * (t + 1)] for t in range(TILES)], axis=0)
        orb_rows[n] = box.astype(BF16)


def base_forward_kernel(orb_rows, y_right, x_left, z_table, coeffs, ends, message, *held):
    for n in range(ORB_DEV):
        box = orb_rows[n].astype(F32)
        forward(box * box, (y_right, x_left, z_table), held[n], coeffs, ends, message, None, n)


def outbox_kernel(chunk, asked, orb_rows, out):
    def step(d, carry):
        out[d, :ROWS, :] = orb_rows[jnp.maximum(asked[d, chunk], 0)]
        return carry

    lax.fori_loop(0, out.shape[0], step, 0)


def pair_forward_kernel(whole, perm, pairs, anchor, orb_rows, fetched, y_right, x_left, z_table, *refs):
    moved_out, coeffs, ends, message, *refs = refs
    energy, *refs = refs if whole else (None, *refs)
    buffers, held = refs[:CHUNK], refs[CHUNK:]
    for n in range(CHUNK):
        clear_margins(buffers[n])
    for n in range(CHUNK):
        _, owner, source, step_x, step_y = pair_scalars(perm, pairs, anchor, n)
        moved = shifted(fetched[source].astype(F32), step_x, step_y, buffers[n])
        moved_out[n] = moved.astype(BF16)
        rho = orb_rows[owner].astype(F32) * moved
        forward(rho, (y_right, x_left, z_table), held[n], coeffs, ends, message, energy, n)
    if whole:
        pack_energy(energy[...], message)


def pair_up(upper, ends, near, z_table, n):
    near_up, near_down = halves(near, n)
    mine = ends[n]
    mine_up, mine_down = mine[:TILES], mine[TILES:]
    low_up = jnp.where(upper, near_up, mine_up)
    high_up = jnp.where(upper, mine_up, near_up)
    low_down = jnp.where(upper, near_down, mine_down)
    high_down = jnp.where(upper, mine_down, near_down)
    up = z_table[PAST_UP] * low_up + high_up
    down = low_down + z_table[PAST_DOWN] * high_down
    return up, down, low_up * high_down


def pair_up_kernel(grid, ends, near, z_table, *outs):
    pair = grid[0] >> 1
    for n in range(CHUNK):
        up, down, _ = pair_up((grid[0] & 1) == 1, ends, near, z_table, n)
        up, down = up.astype(BF16), down.astype(BF16)
        for e in range(1, PAIRS):
            outs[e - 1][n] = jnp.where(pair + e < PAIRS, up, down)


def pair_up_whole_kernel(grid, ends, energy, near, z_table, message):
    rows = lax.broadcasted_iota(jnp.int32, (CHUNK, LANES), 0)
    total = energy[...] + unpack_energy(near)
    for n in range(CHUNK):
        up, down, product = pair_up((grid[0] & 1) == 1, ends, near, z_table, n)
        message[n, :TILES, :] = up.astype(BF16)
        message[n, TILES:, :] = down.astype(BF16)
        total += jnp.where(rows == n, 2.0 * column_sums(z_table[INSIDE] * product), 0.0)
    pack_energy(total, message)


def base_inverse_kernel(grid, near, *refs):
    sums, refs = refs[: PAIRS - 1], refs[PAIRS - 1 :]
    coeffs, orb_rows, y_right, x_left, z_table, total, *held = refs
    for n in range(ORB_DEV):
        here = [block[n].astype(F32) for block in sums]
        potential = inverse(grid[0], near, here, coeffs, (y_right, x_left, z_table), held[n], n)
        total[n] = orb_rows[n].astype(F32) * potential


def pair_inverse_kernel(whole, grid, perm, pairs, anchor, near, *refs):
    count = PAIRS if whole else PAIRS - 1
    blocks, refs = refs[:count], refs[count:]
    coeffs, orb_rows, moved, y_right, x_left, z_table, total_in, total, outbox, *refs = refs
    buffers, held, backs = refs[:CHUNK], refs[CHUNK : 2 * CHUNK], refs[2 * CHUNK]
    pair = grid[0] >> 1
    for n in range(CHUNK):
        clear_margins(buffers[n])
    total[...] = total_in[...]
    if whole:
        within = sum(unpack_energy(block) for block in blocks)
        rows = lax.broadcasted_iota(jnp.int32, (16, LANES), 0)
    for n in range(CHUNK):
        _, owner, _, step_x, step_y = pair_scalars(perm, pairs, anchor, n)
        if whole:
            ends = [halves(block, n) for block in blocks]
            here = [jnp.where(e <= pair, ends[e][0], ends[e][1]) for e in range(1, PAIRS)]
        else:
            here = [block[n].astype(F32) for block in blocks]
        potential = inverse(grid[0], near, here, coeffs, (y_right, x_left, z_table), held[n], n)
        back = shifted(orb_rows[owner].astype(F32) * potential, -step_x, -step_y, buffers[n])
        backs[n, :ROWS, :] = back.astype(BF16)
        if whole:
            value = within[n : n + 1] + between_pairs(pair, ends, z_table)
            high = value.astype(BF16).astype(F32)
            tail = jnp.where(rows == 0, high, jnp.where(rows == 1, value - high, 0.0))
            backs[n, ROWS:, :] = tail.astype(BF16)
    for n in range(CHUNK):
        live, owner, source, _, _ = pair_scalars(perm, pairs, anchor, n)

        @pl.when(live)
        def _():
            outbox[source] = backs[n]
            total[owner] += moved[n].astype(F32) * held[n][...]


def each_arrived(chunk, asked, arrived, action):
    def step(d, carry):
        which = asked[d, chunk]

        @pl.when(which >= 0)
        def _():
            action(which, d)

        return carry

    lax.fori_loop(0, arrived.shape[0], step, 0)


def add_kernel(chunk, asked, arrived, orb_rows, total_in, total, energy):
    total[...] = total_in[...]

    def action(which, d):
        total[which] += arrived[d].astype(F32)

    each_arrived(chunk, asked, arrived, action)
    for n in range(ORB_DEV):
        energy[n : n + 1, :] = column_sums(orb_rows[n].astype(F32) * total[n])


def finish_kernel(chunk, asked, arrived, total_in, energy_in, out, energy_out, total, energy):
    total[...] = total_in[...]
    energy[...] = energy_in[...]

    def action(which, d):
        total[which] += arrived[d, :ROWS, :].astype(F32)
        energy[pl.ds(which, 1), :] += column_sums(arrived[d, ROWS:, :].astype(F32))

    each_arrived(chunk, asked, arrived, action)
    for n in range(ORB_DEV):
        box = total[n]
        out[n] = jnp.concatenate([box[8 * t : 8 * t + 8] for t in range(TILES)], axis=1).astype(BF16)
        energy_out[n] = jnp.sum(energy[n : n + 1, :])


VMEM = pl.BlockSpec(memory_space=pltpu.VMEM)
SMEM = pl.BlockSpec(memory_space=pltpu.SMEM)
HELD = [pltpu.VMEM((ROWS, LANES), F32)] * CHUNK
SHIFT_BUFFERS = [pltpu.VMEM(((2 * PAD + TILES) * 8, LANES), F32)] * CHUNK
MESSAGE = jax.ShapeDtypeStruct((CHUNK, 2 * TILES, LANES), BF16)
MESSAGE_WHOLE = jax.ShapeDtypeStruct((CHUNK + 1, 2 * TILES, LANES), BF16)
SUMS = [jax.ShapeDtypeStruct((CHUNK, TILES, LANES), BF16)] * (PAIRS - 1)
ENDS = jax.ShapeDtypeStruct((CHUNK, 2 * TILES, LANES), F32)
BOXES = jax.ShapeDtypeStruct((CHUNK, ROWS, LANES), BF16)
TOTALS = jax.ShapeDtypeStruct((ORB_DEV, ROWS, LANES), F32)
ENERGY = jax.ShapeDtypeStruct((CHUNK, LANES), F32)


def call(kernel, out_shape, in_specs, scratch, name, micros, out_specs=None, aliases=None):
    return pl.pallas_call(
        kernel,
        out_shape=out_shape,
        in_specs=in_specs,
        out_specs=out_specs if out_specs is not None else jax.tree.map(lambda _: VMEM, out_shape),
        scratch_shapes=scratch,
        input_output_aliases=aliases or {},
        name=name,
        cost_estimate=pl.CostEstimate(flops=0, bytes_accessed=int(micros * 3.0e6), transcendentals=0),
        compiler_params=pltpu.CompilerParams(vmem_limit_bytes=VMEM_LIMIT),
    )


def local(orbitals, pair_list, box_anchor):
    devices = lax.axis_size("orb")
    grid_index = lax.axis_index("grid")
    grid = grid_index.astype(jnp.int32).reshape(1)

    ask, perm = call(
        plan_kernel,
        [
            jax.ShapeDtypeStruct((devices, 1, LANES), jnp.int32),
            jax.ShapeDtypeStruct((2 * CHUNK,), jnp.int32),
        ],
        [SMEM],
        [pltpu.SMEM((devices + 1,), jnp.int32)],
        "plan",
        2,
        out_specs=[VMEM, SMEM],
    )(pair_list)
    asked = lax.all_to_all(ask, "orb", split_axis=0, concat_axis=0, tiled=True).reshape(devices, LANES)

    y_right, x_left = sine_factors()
    z_table = z_factors(grid_index)
    tables = (y_right, x_left, z_table)

    def to_pairs(sums):
        out = [None] * (PAIRS - 1)
        for e in range(1, PAIRS):
            out[e - 1] = lax.ppermute(sums[e - 1], "grid", [(i, (i + 2 * e) % GRID) for i in range(GRID)])
        return out

    def from_grid(ends, message, energy=None):
        near = lax.ppermute(message, "grid", [(i, i ^ 1) for i in range(GRID)])
        if energy is None:
            sums = call(pair_up_kernel, SUMS, [SMEM] + [VMEM] * 3, [], "pair_up", 1)(grid, ends, near, z_table)
            return near, *to_pairs(sums)
        here = call(pair_up_whole_kernel, MESSAGE_WHOLE, [SMEM] + [VMEM] * 4, [], "pair_up_whole", 1)(
            grid, ends, energy, near, z_table
        )
        return near, here, *to_pairs([here] * (PAIRS - 1))

    orb_rows = call(rows_kernel, BOXES, [VMEM], [], "rows", 1)(orbitals)

    def outbox(c):
        shape = jax.ShapeDtypeStruct((devices, ROWS, LANES), BF16)
        return call(functools.partial(outbox_kernel, c), shape, [SMEM, VMEM], [], "outbox", 2)(asked, orb_rows)

    box_a, box_b = outbox(0), outbox(1)
    fetched_a = lax.all_to_all(box_a, "orb", split_axis=0, concat_axis=0, tiled=True)
    base_rows, _ = lax.optimization_barrier((orb_rows, box_a))
    coeffs, *ends = call(
        base_forward_kernel, [TOTALS, ENDS, MESSAGE], [VMEM] * 4, HELD, "base_forward", 3
    )(base_rows, *tables)
    total = call(
        base_inverse_kernel, TOTALS, [SMEM] + [VMEM] * (PAIRS + 5), HELD, "base_inverse", 3
    )(grid, *from_grid(*ends), coeffs, orb_rows, *tables)
    fetched_a, box_b, total = lax.optimization_barrier((fetched_a, box_b, total))
    fetched_b = lax.all_to_all(box_b, "orb", split_axis=0, concat_axis=0, tiled=True)

    def pair_terms(c, fetched, total):
        whole = c == 1
        here = perm[CHUNK * c : CHUNK * (c + 1)]
        moved, coeffs, *ends = call(
            functools.partial(pair_forward_kernel, whole),
            [BOXES, TOTALS, ENDS] + ([MESSAGE_WHOLE, ENERGY] if whole else [MESSAGE]),
            [SMEM] * 3 + [VMEM] * 5,
            SHIFT_BUFFERS + HELD,
            "pair_forward",
            4,
        )(here, pair_list, box_anchor, orb_rows, fetched, *tables)
        blocks = from_grid(*ends)
        rows = ROWS + 16 if whole else ROWS
        return call(
            functools.partial(pair_inverse_kernel, whole),
            [TOTALS, jax.ShapeDtypeStruct((devices, rows, LANES), BF16)],
            [SMEM] * 4 + [VMEM] * (len(blocks) + 7),
            SHIFT_BUFFERS + HELD + [pltpu.VMEM((CHUNK, rows, LANES), BF16)],
            "pair_inverse",
            5,
            aliases={len(blocks) + 10: 0},
        )(grid, here, pair_list, box_anchor, *blocks, coeffs, orb_rows, moved, *tables, total)

    total, back = pair_terms(0, fetched_a, total)
    back, fetched_b = lax.optimization_barrier((back, fetched_b))
    arrived_a = lax.all_to_all(back, "orb", split_axis=0, concat_axis=0, tiled=True)
    total, back = pair_terms(1, fetched_b, total)
    back, arrived_a = lax.optimization_barrier((back, arrived_a))
    arrived_b = lax.all_to_all(back, "orb", split_axis=0, concat_axis=0, tiled=True)
    total, energy = call(
        functools.partial(add_kernel, 0), [TOTALS, ENERGY], [SMEM] + [VMEM] * 3, [], "add", 2, aliases={3: 0}
    )(asked, arrived_a, orb_rows, total)
    energy = lax.psum(energy, "grid")
    total, energy, arrived_b = lax.optimization_barrier((total, energy, arrived_b))
    return call(
        functools.partial(finish_kernel, 1),
        [jax.ShapeDtypeStruct(orbitals.shape, BF16), jax.ShapeDtypeStruct((ORB_DEV,), F32)],
        [SMEM, VMEM, VMEM, VMEM],
        [pltpu.VMEM(TOTALS.shape, F32), pltpu.VMEM(ENERGY.shape, F32)],
        "finish",
        3,
        out_specs=[VMEM, SMEM],
    )(asked, arrived_b, total, energy)


def solution(mesh):
    return jax.shard_map(
        local,
        mesh=mesh,
        in_specs=(P("orb", "grid", None), P(None, "orb"), P()),
        out_specs=(P("orb", "grid", None), P("orb")),
        check_vma=False,
    )
```

```python
import functools

import jax
import jax.numpy as jnp
import ml_dtypes
import numpy as np
from jax import lax
from jax.experimental import pallas as pl
from jax.experimental.pallas import tpu as pltpu
from jax.sharding import PartitionSpec as P

BOX = 64
LANES = 128
TILES = BOX * BOX // LANES
PLANES = 8
ROWS = TILES * PLANES
GRID = 8
PAIRS = GRID // 2
COMBOS = [(p, q) for q in range(PAIRS) for p in range(q)]
PART_ORDER, WHOLE_ORDER = (2, 1, 3), (1, 2, 3)
UP, DOWN, MIDDLE, CARRY, PAST_UP, PAST_DOWN, INSIDE, ACROSS = 0, 8, 16, 24, 27, 28, 29, 30
CHUNK = 8
ORB_DEV = 8
PAD = 10
MU2 = 0.02
BF16 = jnp.bfloat16
F32 = jnp.float32
VMEM_LIMIT = 40 * 1024 * 1024


def sine64():
    steps = np.arange(1, BOX + 1, dtype=np.float64)
    return np.sqrt(2.0 / (BOX + 1)) * np.sin(np.pi * steps[:, None] * steps[None, :] / (BOX + 1))


def high_low(table):
    high = table.astype(np.float32).astype(ml_dtypes.bfloat16)
    rest = table - high.astype(np.float64)
    return high, rest.astype(np.float32).astype(ml_dtypes.bfloat16)


def sine_factors():
    sine = sine64()
    zero = np.zeros((BOX, BOX))
    high, low = high_low(np.block([[sine, zero], [zero, sine]]))
    y_right = np.concatenate(
        [np.concatenate([high, low], 1), np.concatenate([high, np.zeros_like(high)], 1)], 0
    )
    half = 2 * np.arange(TILES)
    rows = []
    for h in range(2):
        rows.append(np.concatenate([sine[np.ix_(half + h, half + h)], sine[np.ix_(half + h, half + 1 - h)]], 1))
    high, low = high_low(np.concatenate(rows, 0))
    return jnp.asarray(y_right), jnp.asarray(np.concatenate([high, high, low], 1))


def z_factors(grid_index):
    steps = jnp.arange(1, BOX + 1).astype(F32)
    eigen = 2.0 - 2.0 * jnp.cos(jnp.pi * steps / (BOX + 1))
    s = (eigen[:, None] + eigen[None, :] + MU2).reshape(TILES, LANES)[None]
    theta = jnp.log(1.0 + 0.5 * s + jnp.sqrt(s + 0.25 * s * s))

    def number(n):
        return jnp.asarray(n).reshape(-1).astype(F32)[:, None, None]

    def rest(n):
        return 1.0 - jnp.exp(-2.0 * theta * number(n))

    def fall(n):
        return jnp.exp(-theta * number(n))

    z = grid_index * PLANES + jnp.arange(PLANES)
    up = fall(1) * rest(z) / rest(z + 1)
    down = fall(1) * rest(63 - z) / rest(64 - z)
    scale = MU2 / (rest(1) * rest(65))
    middle = scale * fall(1) * rest(z + 1) * rest(64 - z)
    pair = grid_index // 2
    e = jnp.arange(1, PAIRS)
    other = (pair - e) % PAIRS
    below = e <= pair
    away = jnp.where(below, 8 * grid_index - 16 * other - 16, 16 * other - 8 * grid_index - 8)
    first = jnp.where(below, 16 * other + 16, 64 - 16 * other)
    last = jnp.where(below, 8 * grid_index, 56 - 8 * grid_index)
    carry = fall(away) * rest(first) / rest(last)
    edge = 16 * pair + 8
    past_up = fall(8) * rest(edge) / rest(edge + 8)
    past_down = fall(8) * rest(64 - edge) / rest(72 - edge)
    inside = scale * fall(2) * rest(edge) * rest(64 - edge)
    m1 = jnp.stack([(pair - p) % PAIRS for p, _ in COMBOS])
    m2 = jnp.stack([(pair - q) % PAIRS for _, q in COMBOS])
    low, high = jnp.minimum(m1, m2), jnp.maximum(m1, m2)
    across = scale * fall(16 * (high - low) - 14) * rest(16 * low + 16) * rest(64 - 16 * high)
    return jnp.concatenate([up, down, middle, carry, past_up, past_down, inside, across], 0)


def lane_iota(rows):
    return lax.broadcasted_iota(jnp.int32, (rows, LANES), 1)


def split(value):
    high = value.astype(BF16)
    return high, (value - high.astype(F32)).astype(BF16)


def dot(left, right):
    return jnp.dot(left, right, preferred_element_type=F32)


def times_y(value, y_right):
    high, low = split(value)
    both = dot(jnp.concatenate([high, low], axis=1), y_right)
    return both[:, :LANES] + both[:, LANES:]


def times_x(planes, x_left, terms):
    value = jnp.concatenate(planes, axis=1)
    other = jnp.concatenate([pltpu.roll(p, BOX, 1) for p in planes], axis=1)
    data = jnp.concatenate([value, other], axis=0)
    if terms == 1:
        high = data.astype(BF16)
        both = dot(x_left[:, BOX:], jnp.concatenate([high, high], axis=0))
    else:
        high, low = split(data)
        both = dot(x_left, jnp.concatenate([high, low, high], axis=0))
    first = lane_iota(TILES) < BOX
    out = []
    for z in range(PLANES):
        tile = both[:, LANES * z : LANES * (z + 1)]
        out.append(jnp.where(first, tile[:TILES], tile[TILES:]))
    return out


def shifted(value, step_x, step_y, buffer):
    buffer[PAD * 8 : PAD * 8 + ROWS, :] = value
    flat = step_x * BOX + step_y
    tiles = flat >> 7
    lanes = flat & 127
    start = pl.multiple_of((tiles + PAD) * 8, 8)
    window = buffer[pl.ds(start, ROWS + 8), :]
    window = pltpu.roll(window, (LANES - lanes) & 127, 1)
    lane = lane_iota(ROWS)
    moved = jnp.where(lane < LANES - lanes, window[:ROWS], window[8:])
    y_new = (lane & (BOX - 1)) + step_y
    return jnp.where((y_new >= 0) & (y_new < BOX), moved, 0.0)


def clear_margins(buffer):
    zero = jnp.zeros((PAD * 8, LANES), F32)
    buffer[: PAD * 8, :] = zero
    buffer[PAD * 8 + ROWS :, :] = zero


def column_sums(value):
    return jnp.sum(value, axis=0, keepdims=True)


def forward(rho, tables, held, coeffs, ends, message, energy, n):
    y_right, x_left, z_table = tables
    held[...] = times_y(rho, y_right[...])
    planes = times_x([held[pl.ds(z, TILES, stride=PLANES), :] for z in range(PLANES)], x_left[...], 1)
    for z in range(PLANES):
        coeffs[n, TILES * z : TILES * (z + 1), :] = planes[z]
    above = jnp.zeros((TILES, LANES), F32)
    product = jnp.zeros((TILES, LANES), F32)
    for z in range(PLANES):
        above = z_table[UP + z] * above + planes[z]
        if energy is not None:
            product += z_table[MIDDLE + z] * planes[z] * (2.0 * above - planes[z])
    below = planes[PLANES - 1]
    for z in range(PLANES - 2, -1, -1):
        below = z_table[DOWN + z] * below + planes[z]
    both = jnp.concatenate([above, below], axis=0)
    ends[n] = both
    message[2 * TILES * n : 2 * TILES * (n + 1), :] = both.astype(BF16)
    if energy is not None:
        energy[n : n + 1, :] = column_sums(product)


def pack_energy(energy, message):
    high = energy.astype(BF16).astype(F32)
    message[2 * TILES * CHUNK :, :] = jnp.concatenate([high, energy - high], axis=0).astype(BF16)


def unpack_energy(message):
    both = message[2 * TILES * CHUNK :, :].astype(F32)
    return both[:8] + both[8:]


def halves(message, n):
    both = message[2 * TILES * n : 2 * TILES * (n + 1), :].astype(F32)
    return both[:TILES], both[TILES:]


def between_pairs(pair, ends, z_table):
    product = jnp.zeros((TILES, LANES), F32)
    for i, (p, q) in enumerate(COMBOS):
        p_low = ((pair - p) & (PAIRS - 1)) < ((pair - q) & (PAIRS - 1))
        low = jnp.where(p_low, ends[p][0], ends[q][0])
        high = jnp.where(p_low, ends[q][1], ends[p][1])
        product += z_table[ACROSS + i] * low * high
    return 2.0 * column_sums(product)


def inverse(grid, near, sums, coeffs, tables, held, n):
    y_right, x_left, z_table = tables
    near_up, near_down = halves(near, n)
    upper = (grid & 1) == 1
    from_below = jnp.where(upper, near_up, 0.0)
    from_above = jnp.where(upper, 0.0, near_down)
    for e in range(1, PAIRS):
        below = e <= (grid >> 1)
        term = z_table[CARRY + e - 1] * sums[e - 1]
        from_below += jnp.where(below, term, 0.0)
        from_above += jnp.where(below, 0.0, term)
    planes = [coeffs[n, TILES * z : TILES * (z + 1), :] for z in range(PLANES)]
    ups = []
    for z in range(PLANES):
        from_below = z_table[UP + z] * from_below + planes[z]
        ups.append(from_below)
    solved = [None] * PLANES
    for z in range(PLANES - 1, -1, -1):
        carried = z_table[DOWN + z] * from_above
        solved[z] = z_table[MIDDLE + z] * (ups[z] + carried)
        from_above = planes[z] + carried
    full = times_y(jnp.concatenate(times_x(solved, x_left[...], 2), axis=0), y_right[...])
    for z in range(PLANES):
        held[pl.ds(z, TILES, stride=PLANES), :] = full[TILES * z : TILES * (z + 1)]
    return held[...]


def pair_scalars(perm, pairs, anchor, n):
    entry = perm[n]
    safe = jnp.maximum(entry, 0)
    owner = pairs[0, safe]
    mate = jnp.maximum(pairs[1, safe], 0)
    step_x = anchor[0, owner] - anchor[0, mate]
    step_y = anchor[1, owner] - anchor[1, mate]
    return entry >= 0, owner & (ORB_DEV - 1), mate >> 3, step_x, step_y


def plan_kernel(pairs, ask, perm, count):
    devices = ask.shape[0]
    entries = 2 * CHUNK
    for t in range(devices + 1):
        count[t] = 0
    for p in range(entries):
        perm[p] = -1
    mates = [pairs[1, p] for p in range(entries)]
    targets = [jnp.where(m >= 0, m >> 3, devices) for m in mates]
    for t in targets:
        count[t] = count[t] + 1
    spots = []
    used = [jnp.int32(0), jnp.int32(0)]
    for p in range(entries):
        seen = count[targets[p]]
        live = mates[p] >= 0
        first, second = live & (seen == 2), live & (seen == 3)
        count[targets[p]] = jnp.where(first, 3, seen)
        spots.append(jnp.where(first, used[0], jnp.where(second, CHUNK + used[1], -1)))
        used[0] += first.astype(jnp.int32)
        used[1] += second.astype(jnp.int32)
    row = lax.broadcasted_iota(jnp.int32, (devices, LANES), 0)
    lane = lax.broadcasted_iota(jnp.int32, (devices, LANES), 1)
    asks = jnp.full((devices, LANES), -1, jnp.int32)
    for p in range(entries):
        live = mates[p] >= 0
        single = live & (spots[p] < 0)
        early = single & (used[0] < CHUNK)
        late = single & (used[0] >= CHUNK)
        spot = jnp.where(early, used[0], jnp.where(late, CHUNK + used[1], spots[p]))
        used[0] += early.astype(jnp.int32)
        used[1] += late.astype(jnp.int32)

        @pl.when(live)
        def _():
            perm[spot] = p

        chunk = jnp.where(spot >= CHUNK, 1, 0)
        here = (row == jnp.where(live, targets[p], -1)) & (lane == chunk)
        asks = jnp.where(here, mates[p] & (ORB_DEV - 1), asks)
    ask[:, 0, :] = asks


def rows_kernel(orb, orb_rows):
    for n in range(ORB_DEV):
        wide = orb[n].astype(F32)
        box = jnp.concatenate([wide[:, LANES * t : LANES * (t + 1)] for t in range(TILES)], axis=0)
        orb_rows[n] = box.astype(BF16)


def base_forward_kernel(orb_rows, y_right, x_left, z_table, coeffs, ends, message, *held):
    for n in range(ORB_DEV):
        box = orb_rows[n].astype(F32)
        forward(box * box, (y_right, x_left, z_table), held[n], coeffs, ends, message, None, n)


def outbox_kernel(chunk, asked, orb_rows, out):
    def step(d, carry):
        out[d, :ROWS, :] = orb_rows[jnp.maximum(asked[d, chunk], 0)]
        return carry

    lax.fori_loop(0, out.shape[0], step, 0)


def pair_forward_kernel(whole, perm, pairs, anchor, orb_rows, fetched, y_right, x_left, z_table, *refs):
    moved_out, coeffs, ends, message, *refs = refs
    energy, *refs = refs if whole else (None, *refs)
    buffers, held = refs[:CHUNK], refs[CHUNK:]
    for n in range(CHUNK):
        clear_margins(buffers[n])
    for n in range(CHUNK):
        _, owner, source, step_x, step_y = pair_scalars(perm, pairs, anchor, n)
        moved = shifted(fetched[source].astype(F32), step_x, step_y, buffers[n])
        moved_out[n] = moved.astype(BF16)
        rho = orb_rows[owner].astype(F32) * moved
        forward(rho, (y_right, x_left, z_table), held[n], coeffs, ends, message, energy, n)
    if whole:
        pack_energy(energy[...], message)


def pair_up(upper, ends, near, z_table, n):
    near_up, near_down = halves(near, n)
    mine = ends[n]
    mine_up, mine_down = mine[:TILES], mine[TILES:]
    low_up = jnp.where(upper, near_up, mine_up)
    high_up = jnp.where(upper, mine_up, near_up)
    low_down = jnp.where(upper, near_down, mine_down)
    high_down = jnp.where(upper, mine_down, near_down)
    up = z_table[PAST_UP] * low_up + high_up
    down = low_down + z_table[PAST_DOWN] * high_down
    return up, down, low_up * high_down


def pair_up_kernel(grid, ends, near, z_table, *outs):
    pair = grid[0] >> 1
    for n in range(CHUNK):
        up, down, _ = pair_up((grid[0] & 1) == 1, ends, near, z_table, n)
        up, down = up.astype(BF16), down.astype(BF16)
        for e in range(1, PAIRS):
            outs[e - 1][n] = jnp.where(pair + e < PAIRS, up, down)


def pair_up_whole_kernel(grid, ends, energy, near, z_table, message):
    rows = lax.broadcasted_iota(jnp.int32, (CHUNK, LANES), 0)
    total = energy[...] + unpack_energy(near)
    for n in range(CHUNK):
        up, down, product = pair_up((grid[0] & 1) == 1, ends, near, z_table, n)
        both = jnp.concatenate([up, down], axis=0)
        message[2 * TILES * n : 2 * TILES * (n + 1), :] = both.astype(BF16)
        total += jnp.where(rows == n, 2.0 * column_sums(z_table[INSIDE] * product), 0.0)
    pack_energy(total, message)


def in_order(refs, order):
    return [refs[order.index(e)] for e in range(1, PAIRS)]


def base_inverse_kernel(grid, near, *refs):
    sums, refs = in_order(refs[: PAIRS - 1], PART_ORDER), refs[PAIRS - 1 :]
    coeffs, orb_rows, y_right, x_left, z_table, total, *held = refs
    for n in range(ORB_DEV):
        here = [block[n].astype(F32) for block in sums]
        potential = inverse(grid[0], near, here, coeffs, (y_right, x_left, z_table), held[n], n)
        total[n] = orb_rows[n].astype(F32) * potential


def pair_inverse_kernel(whole, grid, perm, pairs, anchor, near, *refs):
    count = PAIRS if whole else PAIRS - 1
    blocks, refs = refs[:count], refs[count:]
    if whole:
        blocks = [blocks[0], *in_order(blocks[1:], WHOLE_ORDER)]
    else:
        blocks = in_order(blocks, PART_ORDER)
    coeffs, orb_rows, moved, y_right, x_left, z_table, total_in, total, outbox, *refs = refs
    buffers, held, backs = refs[:CHUNK], refs[CHUNK : 2 * CHUNK], refs[2 * CHUNK]
    pair = grid[0] >> 1
    for n in range(CHUNK):
        clear_margins(buffers[n])
    total[...] = total_in[...]
    if whole:
        within = sum(unpack_energy(block) for block in blocks)
        rows = lax.broadcasted_iota(jnp.int32, (16, LANES), 0)
    for n in range(CHUNK):
        _, owner, _, step_x, step_y = pair_scalars(perm, pairs, anchor, n)
        if whole:
            ends = [halves(block, n) for block in blocks]
            here = [jnp.where(e <= pair, ends[e][0], ends[e][1]) for e in range(1, PAIRS)]
        else:
            here = [block[n].astype(F32) for block in blocks]
        potential = inverse(grid[0], near, here, coeffs, (y_right, x_left, z_table), held[n], n)
        back = shifted(orb_rows[owner].astype(F32) * potential, -step_x, -step_y, buffers[n])
        backs[n, :ROWS, :] = back.astype(BF16)
        if whole:
            value = within[n : n + 1] + between_pairs(pair, ends, z_table)
            high = value.astype(BF16).astype(F32)
            tail = jnp.where(rows == 0, high, jnp.where(rows == 1, value - high, 0.0))
            backs[n, ROWS:, :] = tail.astype(BF16)
    for n in range(CHUNK):
        live, owner, source, _, _ = pair_scalars(perm, pairs, anchor, n)

        @pl.when(live)
        def _():
            outbox[source] = backs[n]
            total[owner] += moved[n].astype(F32) * held[n][...]


def each_arrived(asked, arrived, action):
    def step(d, carry):
        which = asked[d]

        @pl.when(which >= 0)
        def _():
            action(which, d)

        return carry

    lax.fori_loop(0, arrived.shape[0], step, 0)


def add_kernel(asked, arrived, orb_rows, total_in, total, energy):
    total[...] = total_in[...]

    def action(which, d):
        total[which] += arrived[d].astype(F32)

    each_arrived(asked, arrived, action)
    for n in range(ORB_DEV):
        energy[n : n + 1, :] = column_sums(orb_rows[n].astype(F32) * total[n])


def finish_kernel(asked, arrived, total_in, energy_in, out, energy_out, total, energy, boxes, sems):
    count = arrived.shape[0]
    which = [asked[d] for d in range(count)]
    copies = [pltpu.make_async_copy(arrived.at[d], boxes.at[d], sems.at[d]) for d in range(count)]
    for d in range(count):

        @pl.when(which[d] >= 0)
        def _():
            copies[d].start()

    total[...] = total_in[...]
    energy[...] = energy_in[...]
    for d in range(count):

        @pl.when(which[d] >= 0)
        def _():
            copies[d].wait()
            total[which[d]] += boxes[d, :ROWS, :].astype(F32)
            energy[pl.ds(which[d], 1), :] += column_sums(boxes[d, ROWS:, :].astype(F32))

    for n in range(ORB_DEV):
        box = total[n]
        out[n] = jnp.concatenate([box[8 * t : 8 * t + 8] for t in range(TILES)], axis=1).astype(BF16)
        energy_out[n] = jnp.sum(energy[n : n + 1, :])


VMEM = pl.BlockSpec(memory_space=pltpu.VMEM)
SMEM = pl.BlockSpec(memory_space=pltpu.SMEM)
ANY = pl.BlockSpec(memory_space=pl.ANY)
HELD = [pltpu.VMEM((ROWS, LANES), F32)] * CHUNK
SHIFT_BUFFERS = [pltpu.VMEM(((2 * PAD + TILES) * 8, LANES), F32)] * CHUNK
MESSAGE = jax.ShapeDtypeStruct((CHUNK * 2 * TILES, LANES), BF16)
MESSAGE_WHOLE = jax.ShapeDtypeStruct((CHUNK * 2 * TILES + 16, LANES), BF16)
SUMS = [jax.ShapeDtypeStruct((CHUNK, TILES, LANES), BF16)] * (PAIRS - 1)
ENDS = jax.ShapeDtypeStruct((CHUNK, 2 * TILES, LANES), F32)
BOXES = jax.ShapeDtypeStruct((CHUNK, ROWS, LANES), BF16)
TOTALS = jax.ShapeDtypeStruct((ORB_DEV, ROWS, LANES), F32)
ENERGY = jax.ShapeDtypeStruct((CHUNK, LANES), F32)


def call(kernel, out_shape, in_specs, scratch, name, micros, out_specs=None, aliases=None):
    return pl.pallas_call(
        kernel,
        out_shape=out_shape,
        in_specs=in_specs,
        out_specs=out_specs if out_specs is not None else jax.tree.map(lambda _: VMEM, out_shape),
        scratch_shapes=scratch,
        input_output_aliases=aliases or {},
        name=name,
        cost_estimate=pl.CostEstimate(flops=0, bytes_accessed=int(micros * 3.0e6), transcendentals=0),
        compiler_params=pltpu.CompilerParams(vmem_limit_bytes=VMEM_LIMIT),
    )


def local(orbitals, pair_list, box_anchor):
    devices = lax.axis_size("orb")
    grid_index = lax.axis_index("grid")
    grid = grid_index.astype(jnp.int32).reshape(1)

    ask, perm = call(
        plan_kernel,
        [
            jax.ShapeDtypeStruct((devices, 1, LANES), jnp.int32),
            jax.ShapeDtypeStruct((2 * CHUNK,), jnp.int32),
        ],
        [SMEM],
        [pltpu.SMEM((devices + 1,), jnp.int32)],
        "plan",
        2,
        out_specs=[VMEM, SMEM],
    )(pair_list)
    asked = lax.all_to_all(ask, "orb", split_axis=0, concat_axis=0, tiled=True).reshape(devices, LANES)

    y_right, x_left = sine_factors()
    z_table = z_factors(grid_index)
    tables = (y_right, x_left, z_table)

    def to_pairs(sums, order):
        return [
            lax.ppermute(sums[e - 1], "grid", [(i, (i + 2 * e) % GRID) for i in range(GRID)]) for e in order
        ]

    def from_grid(ends, message, energy=None):
        near = lax.ppermute(message, "grid", [(i, i ^ 1) for i in range(GRID)])
        if energy is None:
            sums = call(pair_up_kernel, SUMS, [SMEM] + [VMEM] * 3, [], "pair_up", 1)(grid, ends, near, z_table)
            return near, *to_pairs(sums, PART_ORDER)
        here = call(pair_up_whole_kernel, MESSAGE_WHOLE, [SMEM] + [VMEM] * 4, [], "pair_up_whole", 1)(
            grid, ends, energy, near, z_table
        )
        return near, here, *to_pairs([here] * (PAIRS - 1), WHOLE_ORDER)

    orb_rows = call(rows_kernel, BOXES, [VMEM], [], "rows", 1)(orbitals)

    def outbox(c):
        shape = jax.ShapeDtypeStruct((devices, ROWS, LANES), BF16)
        return call(functools.partial(outbox_kernel, c), shape, [SMEM, VMEM], [], "outbox", 2)(asked, orb_rows)

    box_a, box_b = outbox(0), outbox(1)
    fetched_a = lax.all_to_all(box_a, "orb", split_axis=0, concat_axis=0, tiled=True)
    base_rows, _ = lax.optimization_barrier((orb_rows, box_a))
    coeffs, *ends = call(
        base_forward_kernel, [TOTALS, ENDS, MESSAGE], [VMEM] * 4, HELD, "base_forward", 3
    )(base_rows, *tables)
    total = call(
        base_inverse_kernel, TOTALS, [SMEM] + [VMEM] * (PAIRS + 5), HELD, "base_inverse", 3
    )(grid, *from_grid(*ends), coeffs, orb_rows, *tables)
    fetched_a, box_b, total = lax.optimization_barrier((fetched_a, box_b, total))
    fetched_b = lax.all_to_all(box_b, "orb", split_axis=0, concat_axis=0, tiled=True)

    def pair_terms(c, fetched, total):
        whole = c == 1
        here = perm[CHUNK * c : CHUNK * (c + 1)]
        moved, coeffs, *ends = call(
            functools.partial(pair_forward_kernel, whole),
            [BOXES, TOTALS, ENDS] + ([MESSAGE_WHOLE, ENERGY] if whole else [MESSAGE]),
            [SMEM] * 3 + [VMEM] * 5,
            SHIFT_BUFFERS + HELD,
            "pair_forward",
            4,
        )(here, pair_list, box_anchor, orb_rows, fetched, *tables)
        blocks = from_grid(*ends)
        rows = ROWS + 16 if whole else ROWS
        return call(
            functools.partial(pair_inverse_kernel, whole),
            [TOTALS, jax.ShapeDtypeStruct((devices, rows, LANES), BF16)],
            [SMEM] * 4 + [VMEM] * (len(blocks) + 7),
            SHIFT_BUFFERS + HELD + [pltpu.VMEM((CHUNK, rows, LANES), BF16)],
            "pair_inverse",
            5,
            aliases={len(blocks) + 10: 0},
        )(grid, here, pair_list, box_anchor, *blocks, coeffs, orb_rows, moved, *tables, total)

    total, back = pair_terms(0, fetched_a, total)
    back, fetched_b = lax.optimization_barrier((back, fetched_b))
    arrived_a = lax.all_to_all(back, "orb", split_axis=0, concat_axis=0, tiled=True)
    total, back = pair_terms(1, fetched_b, total)
    back, arrived_a = lax.optimization_barrier((back, arrived_a))
    arrived_b = lax.all_to_all(back, "orb", split_axis=0, concat_axis=0, tiled=True)
    total, energy = call(
        add_kernel, [TOTALS, ENERGY], [SMEM] + [VMEM] * 3, [], "add", 2, aliases={3: 0}
    )(asked[:, 0], arrived_a, orb_rows, total)
    energy = lax.psum(energy, "grid")
    asked_b, total, energy, arrived_b = lax.optimization_barrier((asked[:, 1], total, energy, arrived_b))
    return call(
        finish_kernel,
        [jax.ShapeDtypeStruct(orbitals.shape, BF16), jax.ShapeDtypeStruct((ORB_DEV,), F32)],
        [SMEM, ANY, VMEM, VMEM],
        [
            pltpu.VMEM(TOTALS.shape, F32),
            pltpu.VMEM(ENERGY.shape, F32),
            pltpu.VMEM(arrived_b.shape, BF16),
            pltpu.SemaphoreType.DMA((devices,)),
        ],
        "finish",
        3,
        out_specs=[VMEM, SMEM],
    )(asked_b, arrived_b, total, energy)


def solution(mesh):
    return jax.shard_map(
        local,
        mesh=mesh,
        in_specs=(P("orb", "grid", None), P(None, "orb"), P()),
        out_specs=(P("orb", "grid", None), P("orb")),
        check_vma=False,
    )
```

```python
import functools

import jax
import jax.numpy as jnp
import ml_dtypes
import numpy as np
from jax import lax
from jax.experimental import pallas as pl
from jax.experimental.pallas import tpu as pltpu
from jax.sharding import PartitionSpec as P

BOX = 64
LANES = 128
TILES = BOX * BOX // LANES
PLANES = 8
ROWS = TILES * PLANES
GRID = 8
PAIRS = GRID // 2
ORDER = (2, 1, 3)
UP, DOWN, MIDDLE, CARRY, PAST_UP, PAST_DOWN = 0, 8, 16, 24, 27, 28
ORB_DEV = 8
ENTRIES = 16
PAD = 10
MU2 = 0.02
BF16 = jnp.bfloat16
F32 = jnp.float32
VMEM_LIMIT = 40 * 1024 * 1024


def sine64():
    steps = np.arange(1, BOX + 1, dtype=np.float64)
    return np.sqrt(2.0 / (BOX + 1)) * np.sin(np.pi * steps[:, None] * steps[None, :] / (BOX + 1))


def high_low(table):
    high = table.astype(np.float32).astype(ml_dtypes.bfloat16)
    rest = table - high.astype(np.float64)
    return high, rest.astype(np.float32).astype(ml_dtypes.bfloat16)


def sine_factors():
    sine = sine64()
    zero = np.zeros((BOX, BOX))
    high, low = high_low(np.block([[sine, zero], [zero, sine]]))
    y_right = np.concatenate(
        [np.concatenate([high, low], 1), np.concatenate([high, np.zeros_like(high)], 1)], 0
    )
    half = 2 * np.arange(TILES)
    rows = []
    for h in range(2):
        rows.append(np.concatenate([sine[np.ix_(half + h, half + h)], sine[np.ix_(half + h, half + 1 - h)]], 1))
    high, low = high_low(np.concatenate(rows, 0))
    return jnp.asarray(y_right), jnp.asarray(np.concatenate([high, high, low], 1))


def z_factors(grid_index):
    steps = jnp.arange(1, BOX + 1).astype(F32)
    eigen = 2.0 - 2.0 * jnp.cos(jnp.pi * steps / (BOX + 1))
    s = (eigen[:, None] + eigen[None, :] + MU2).reshape(TILES, LANES)[None]
    theta = jnp.log(1.0 + 0.5 * s + jnp.sqrt(s + 0.25 * s * s))

    def number(n):
        return jnp.asarray(n).reshape(-1).astype(F32)[:, None, None]

    def rest(n):
        return 1.0 - jnp.exp(-2.0 * theta * number(n))

    def fall(n):
        return jnp.exp(-theta * number(n))

    z = grid_index * PLANES + jnp.arange(PLANES)
    up = fall(1) * rest(z) / rest(z + 1)
    down = fall(1) * rest(63 - z) / rest(64 - z)
    scale = MU2 / (rest(1) * rest(65))
    middle = scale * fall(1) * rest(z + 1) * rest(64 - z)
    pair = grid_index // 2
    e = jnp.arange(1, PAIRS)
    other = (pair - e) % PAIRS
    below = e <= pair
    away = jnp.where(below, 8 * grid_index - 16 * other - 16, 16 * other - 8 * grid_index - 8)
    first = jnp.where(below, 16 * other + 16, 64 - 16 * other)
    last = jnp.where(below, 8 * grid_index, 56 - 8 * grid_index)
    carry = fall(away) * rest(first) / rest(last)
    edge = 16 * pair + 8
    past_up = fall(8) * rest(edge) / rest(edge + 8)
    past_down = fall(8) * rest(64 - edge) / rest(72 - edge)
    return jnp.concatenate([up, down, middle, carry, past_up, past_down], 0)


def lane_iota(rows):
    return lax.broadcasted_iota(jnp.int32, (rows, LANES), 1)


def split(value):
    high = value.astype(BF16)
    return high, (value - high.astype(F32)).astype(BF16)


def dot(left, right):
    return jnp.dot(left, right, preferred_element_type=F32)


def times_y(value, y_right):
    high, low = split(value)
    both = dot(jnp.concatenate([high, low], axis=1), y_right)
    return both[:, :LANES] + both[:, LANES:]


def times_x(planes, x_left, terms):
    value = jnp.concatenate(planes, axis=1)
    other = jnp.concatenate([pltpu.roll(p, BOX, 1) for p in planes], axis=1)
    data = jnp.concatenate([value, other], axis=0)
    if terms == 1:
        high = data.astype(BF16)
        both = dot(x_left[:, BOX:], jnp.concatenate([high, high], axis=0))
    else:
        high, low = split(data)
        both = dot(x_left, jnp.concatenate([high, low, high], axis=0))
    first = lane_iota(TILES) < BOX
    out = []
    for z in range(PLANES):
        tile = both[:, LANES * z : LANES * (z + 1)]
        out.append(jnp.where(first, tile[:TILES], tile[TILES:]))
    return out


def shifted(value, step_x, step_y, buffer):
    buffer[PAD * 8 : PAD * 8 + ROWS, :] = value
    flat = step_x * BOX + step_y
    tiles = flat >> 7
    lanes = flat & 127
    start = pl.multiple_of((tiles + PAD) * 8, 8)
    window = buffer[pl.ds(start, ROWS + 8), :]
    window = pltpu.roll(window, (LANES - lanes) & 127, 1)
    lane = lane_iota(ROWS)
    moved = jnp.where(lane < LANES - lanes, window[:ROWS], window[8:])
    y_new = (lane & (BOX - 1)) + step_y
    return jnp.where((y_new >= 0) & (y_new < BOX), moved, 0.0)


def clear_margins(buffer):
    zero = jnp.zeros((PAD * 8, LANES), F32)
    buffer[: PAD * 8, :] = zero
    buffer[PAD * 8 + ROWS :, :] = zero


def column_sums(value):
    return jnp.sum(value, axis=0, keepdims=True)


def forward(rho, tables, held, coeffs, ends, message, n):
    y_right, x_left, z_table = tables
    held[...] = times_y(rho, y_right[...])
    planes = times_x([held[pl.ds(z, TILES, stride=PLANES), :] for z in range(PLANES)], x_left[...], 1)
    for z in range(PLANES):
        coeffs[n, TILES * z : TILES * (z + 1), :] = planes[z]
    above = planes[0]
    for z in range(1, PLANES):
        above = z_table[UP + z] * above + planes[z]
    below = planes[PLANES - 1]
    for z in range(PLANES - 2, -1, -1):
        below = z_table[DOWN + z] * below + planes[z]
    both = jnp.concatenate([above, below], axis=0)
    ends[n] = both
    message[2 * TILES * n : 2 * TILES * (n + 1), :] = both.astype(BF16)


def halves(message, n):
    both = message[2 * TILES * n : 2 * TILES * (n + 1), :].astype(F32)
    return both[:TILES], both[TILES:]


def inverse(grid, near, sums, coeffs, tables, held, n):
    y_right, x_left, z_table = tables
    near_up, near_down = halves(near, n)
    upper = (grid & 1) == 1
    from_below = jnp.where(upper, near_up, 0.0)
    from_above = jnp.where(upper, 0.0, near_down)
    for e in range(1, PAIRS):
        below = e <= (grid >> 1)
        term = z_table[CARRY + e - 1] * sums[e - 1]
        from_below += jnp.where(below, term, 0.0)
        from_above += jnp.where(below, 0.0, term)
    planes = [coeffs[n, TILES * z : TILES * (z + 1), :] for z in range(PLANES)]
    ups = []
    for z in range(PLANES):
        from_below = z_table[UP + z] * from_below + planes[z]
        ups.append(from_below)
    solved = [None] * PLANES
    product = jnp.zeros((TILES, LANES), F32)
    for z in range(PLANES - 1, -1, -1):
        carried = z_table[DOWN + z] * from_above
        solved[z] = z_table[MIDDLE + z] * (ups[z] + carried)
        from_above = planes[z] + carried
        product += planes[z] * solved[z]
    full = times_y(jnp.concatenate(times_x(solved, x_left[...], 2), axis=0), y_right[...])
    for z in range(PLANES):
        held[pl.ds(z, TILES, stride=PLANES), :] = full[TILES * z : TILES * (z + 1)]
    return held[...], column_sums(product)


def pair_scalars(pairs, anchor, n):
    owner = pairs[0, n]
    mate = jnp.maximum(pairs[1, n], 0)
    step_x = anchor[0, owner] - anchor[0, mate]
    step_y = anchor[1, owner] - anchor[1, mate]
    return pairs[1, n] >= 0, owner & (ORB_DEV - 1), step_x, step_y


def tile(box, t):
    return box[PLANES * t : PLANES * (t + 1)]


def spread_kernel(pairs, orb, orb_rows, out):
    wide = [orb[n].astype(F32) for n in range(ORB_DEV)]
    for n in range(ORB_DEV):
        box = jnp.concatenate([wide[n][:, LANES * t : LANES * (t + 1)] for t in range(TILES)], axis=0)
        orb_rows[n] = box.astype(BF16)
    rows = lax.broadcasted_iota(jnp.int32, (ENTRIES, LANES), 0)
    partners = jnp.zeros((ENTRIES, LANES), F32)
    for n in range(ENTRIES):
        partners = jnp.where(rows == n, pairs[1, n].astype(F32), partners)
    partners = partners.astype(BF16)
    for t in range(TILES):
        piece = jnp.concatenate([w[:, LANES * t : LANES * (t + 1)] for w in wide], axis=0)
        out[t, : ORB_DEV * PLANES, :] = piece.astype(BF16)
        out[t, ORB_DEV * PLANES :, :] = partners


def serve_kernel(partners, held, out, every):
    count = held.shape[0]
    for d in range(count):
        pieces = held[d, : ORB_DEV * PLANES, :].astype(F32)
        for n in range(ORB_DEV):
            every[ORB_DEV * d + n] = tile(pieces, n)

    def step(d, carry):
        pieces = [every[jnp.maximum(partners[ENTRIES * d + n], 0)] for n in range(ENTRIES)]
        out[d] = jnp.concatenate(pieces, axis=0).astype(BF16)
        return carry

    lax.fori_loop(0, count, step, 0)


def base_forward_kernel(orb_rows, y_right, x_left, z_table, coeffs, ends, message, *held):
    for n in range(ORB_DEV):
        box = orb_rows[n].astype(F32)
        forward(box * box, (y_right, x_left, z_table), held[n], coeffs, ends, message, n)


def pair_forward_kernel(pairs, anchor, orb_rows, fetched, y_right, x_left, z_table, moved_out, coeffs, ends, message, *refs):
    buffers, held = refs[:ENTRIES], refs[ENTRIES:]
    for n in range(ENTRIES):
        clear_margins(buffers[n])
    for m in range(0, ENTRIES, 2):
        both = [fetched[t, PLANES * m : PLANES * (m + 2), :].astype(F32) for t in range(TILES)]
        for n in (m, m + 1):
            _, owner, step_x, step_y = pair_scalars(pairs, anchor, n)
            mate = jnp.concatenate([tile(b, n - m) for b in both], axis=0)
            moved = shifted(mate, step_x, step_y, buffers[n])
            moved_out[n] = moved.astype(BF16)
            rho = orb_rows[owner].astype(F32) * moved
            forward(rho, (y_right, x_left, z_table), held[n], coeffs, ends, message, n)


def pair_up_kernel(grid, ends, near, z_table, *outs):
    pair, upper = grid[0] >> 1, (grid[0] & 1) == 1
    for n in range(ends.shape[0]):
        near_up, near_down = halves(near, n)
        mine = ends[n]
        mine_up, mine_down = mine[:TILES], mine[TILES:]
        low_up = jnp.where(upper, near_up, mine_up)
        high_up = jnp.where(upper, mine_up, near_up)
        low_down = jnp.where(upper, near_down, mine_down)
        high_down = jnp.where(upper, mine_down, near_down)
        up = (z_table[PAST_UP] * low_up + high_up).astype(BF16)
        down = (low_down + z_table[PAST_DOWN] * high_down).astype(BF16)
        for e in range(1, PAIRS):
            outs[e - 1][n] = jnp.where(pair + e < PAIRS, up, down)


def in_order(refs, n):
    return [refs[ORDER.index(e)][n].astype(F32) for e in range(1, PAIRS)]


def base_inverse_kernel(grid, near, *refs):
    sums, refs = refs[: PAIRS - 1], refs[PAIRS - 1 :]
    coeffs, orb_rows, y_right, x_left, z_table, total, energy, *held = refs
    tables = (y_right, x_left, z_table)
    for n in range(ORB_DEV):
        potential, value = inverse(grid[0], near, in_order(sums, n), coeffs, tables, held[n], n)
        total[n] = orb_rows[n].astype(F32) * potential
        energy[n : n + 1, :] = value


def pair_inverse_kernel(grid, pairs, anchor, near, *refs):
    sums, refs = refs[: PAIRS - 1], refs[PAIRS - 1 :]
    coeffs, orb_rows, moved, y_right, x_left, z_table, total_in, total, energy, out, *refs = refs
    buffers, held = refs[:ENTRIES], refs[ENTRIES:]
    tables = (y_right, x_left, z_table)
    for n in range(ENTRIES):
        clear_margins(buffers[n])
    total[...] = total_in[...]
    for m in range(0, ENTRIES, 2):
        backs = []
        for n in (m, m + 1):
            _, owner, step_x, step_y = pair_scalars(pairs, anchor, n)
            potential, value = inverse(grid[0], near, in_order(sums, n), coeffs, tables, held[n], n)
            energy[n : n + 1, :] = value
            backs.append(shifted(orb_rows[owner].astype(F32) * potential, -step_x, -step_y, buffers[n]))
        for t in range(TILES):
            piece = jnp.concatenate([tile(back, t) for back in backs], axis=0)
            out[t, PLANES * m : PLANES * (m + 2), :] = piece.astype(BF16)
    for n in range(ENTRIES):
        live, owner, _, _ = pair_scalars(pairs, anchor, n)
        total[owner] += jnp.where(live, moved[n].astype(F32) * held[n][...], 0.0)


def gather_kernel(partners, pairs, arrived, energy, out, energy_here, every_energy, *every):
    count = arrived.shape[0]
    spare = ORB_DEV * count
    for part in every:
        part[...] = jnp.zeros_like(part)

    def step(d, carry):
        for m in range(0, ENTRIES, 2):
            both = arrived[d, PLANES * m : PLANES * (m + 2), :].astype(F32)
            for n in (m, m + 1):
                which = partners[ENTRIES * d + n]
                which = jnp.where(which >= 0, which, spare)
                every[n % len(every)][which] += tile(both, n - m)
        return carry

    lax.fori_loop(0, count, step, 0)
    every_energy[...] = jnp.zeros_like(every_energy)
    first = lane_iota(1) == 0
    for n in range(ORB_DEV):
        energy_here[n : n + 1, :] = jnp.where(first, energy[n], 0.0)
    for n in range(ENTRIES):
        mate = pairs[1, n]
        owner = pairs[0, n] & (ORB_DEV - 1)
        value = jnp.where(first & (mate >= 0), energy[ORB_DEV + n], 0.0)
        every_energy[pl.ds(jnp.where(mate >= 0, mate, spare), 1), :] += value
        energy_here[pl.ds(owner, 1), :] += value
    for d in range(count):
        pieces = [sum(part[ORB_DEV * d + n] for part in every) for n in range(ORB_DEV)]
        out[d, : ORB_DEV * PLANES, :] = jnp.concatenate(pieces, axis=0).astype(BF16)
        value = every_energy[ORB_DEV * d : ORB_DEV * (d + 1), :]
        high = value.astype(BF16).astype(F32)
        out[d, ORB_DEV * PLANES :, :] = jnp.concatenate([high, value - high], axis=0).astype(BF16)


def finish_kernel(arrived, total, energy, out, energy_out):
    sums = energy[...]
    for t in range(TILES):
        pieces = arrived[t, : ORB_DEV * PLANES, :].astype(F32)
        for n in range(ORB_DEV):
            here = total[n, PLANES * t : PLANES * (t + 1), :] + tile(pieces, n)
            out[n, :, LANES * t : LANES * (t + 1)] = here.astype(BF16)
        both = arrived[t, ORB_DEV * PLANES :, :].astype(F32)
        sums += both[:ORB_DEV] + both[ORB_DEV:]
    for n in range(ORB_DEV):
        energy_out[n] = jnp.sum(sums[n : n + 1, :])


VMEM = pl.BlockSpec(memory_space=pltpu.VMEM)
SMEM = pl.BlockSpec(memory_space=pltpu.SMEM)
HELD = pltpu.VMEM((ROWS, LANES), F32)
SHIFT_BUFFER = pltpu.VMEM(((2 * PAD + TILES) * 8, LANES), F32)


def shape(*dims, dtype=BF16):
    return jax.ShapeDtypeStruct(dims, dtype)


def solve_shapes(count):
    return [
        shape(count, ROWS, LANES, dtype=F32),
        shape(count, 2 * TILES, LANES, dtype=F32),
        shape(count * 2 * TILES, LANES),
    ]


def call(kernel, out_shape, in_specs, scratch, name, micros, out_specs=None, aliases=None):
    return pl.pallas_call(
        kernel,
        out_shape=out_shape,
        in_specs=in_specs,
        out_specs=out_specs if out_specs is not None else jax.tree.map(lambda _: VMEM, out_shape),
        scratch_shapes=scratch,
        input_output_aliases=aliases or {},
        name=name,
        cost_estimate=pl.CostEstimate(flops=0, bytes_accessed=int(micros * 3.0e6), transcendentals=0),
        compiler_params=pltpu.CompilerParams(vmem_limit_bytes=VMEM_LIMIT),
    )


def local(orbitals, pair_list, box_anchor):
    devices = lax.axis_size("orb")
    grid_index = lax.axis_index("grid")
    grid = grid_index.astype(jnp.int32).reshape(1)
    y_right, x_left = sine_factors()
    z_table = z_factors(grid_index)
    tables = (y_right, x_left, z_table)
    spread = ORB_DEV * PLANES + ENTRIES
    totals = shape(ORB_DEV, ROWS, LANES, dtype=F32)

    def to_all(blocks):
        return lax.all_to_all(blocks, "orb", split_axis=0, concat_axis=0, tiled=True)

    def to_near(message):
        return lax.ppermute(message, "grid", [(i, i ^ 1) for i in range(GRID)])

    def from_pairs(ends, near):
        outs = [shape(ends.shape[0], TILES, LANES)] * (PAIRS - 1)
        sums = call(pair_up_kernel, outs, [SMEM] + [VMEM] * 3, [], "pair_up", 1)(grid, ends, near, z_table)
        hops = [[(i, (i + 2 * e) % GRID) for i in range(GRID)] for e in ORDER]
        return [lax.ppermute(sums[e - 1], "grid", hop) for e, hop in zip(ORDER, hops)]

    orb_rows, pieces = call(
        spread_kernel,
        [shape(ORB_DEV, ROWS, LANES), shape(devices, spread, LANES)],
        [SMEM, VMEM],
        [],
        "spread",
        2,
    )(pair_list, orbitals)
    pieces = to_all(pieces)
    base_coeffs, base_ends, message = call(
        base_forward_kernel, solve_shapes(ORB_DEV), [VMEM] * 4, [HELD] * ORB_DEV, "base_forward", 2
    )(orb_rows, *tables)
    pieces, base_near = lax.optimization_barrier((pieces, to_near(message)))
    partners = pieces[:, ORB_DEV * PLANES :, 0].astype(jnp.int32).reshape(-1)
    served = call(
        serve_kernel,
        shape(devices, ENTRIES * PLANES, LANES),
        [SMEM, VMEM],
        [pltpu.VMEM((devices * ORB_DEV, PLANES, LANES), F32)],
        "serve",
        2,
    )(partners, pieces)
    fetched = to_all(served)
    total, base_energy = call(
        base_inverse_kernel,
        [totals, shape(ORB_DEV, LANES, dtype=F32)],
        [SMEM] + [VMEM] * (PAIRS + 5),
        [HELD] * ORB_DEV,
        "base_inverse",
        2,
    )(grid, base_near, *from_pairs(base_ends, base_near), base_coeffs, orb_rows, *tables)
    fetched, total = lax.optimization_barrier((fetched, total))

    moved, coeffs, ends, message = call(
        pair_forward_kernel,
        [shape(ENTRIES, ROWS, LANES)] + solve_shapes(ENTRIES),
        [SMEM] * 2 + [VMEM] * 5,
        [SHIFT_BUFFER] * ENTRIES + [HELD] * ENTRIES,
        "pair_forward",
        5,
    )(pair_list, box_anchor, orb_rows, fetched, *tables)
    near = to_near(message)
    total, pair_energy, back = call(
        pair_inverse_kernel,
        [totals, shape(ENTRIES, LANES, dtype=F32), shape(devices, ENTRIES * PLANES, LANES)],
        [SMEM] * 3 + [VMEM] * (PAIRS + 7),
        [SHIFT_BUFFER] * ENTRIES + [HELD] * ENTRIES,
        "pair_inverse",
        5,
        aliases={PAIRS + 9: 0},
    )(grid, pair_list, box_anchor, near, *from_pairs(ends, near), coeffs, orb_rows, moved, *tables, total)

    arrived = to_all(back)
    energy = lax.psum(jnp.sum(jnp.concatenate([base_energy, pair_energy]), axis=1), "grid")
    due, energy = call(
        gather_kernel,
        [shape(devices, spread, LANES), shape(ORB_DEV, LANES, dtype=F32)],
        [SMEM] * 2 + [VMEM, SMEM],
        [pltpu.VMEM((devices * ORB_DEV + 8, LANES), F32)]
        + [pltpu.VMEM((devices * ORB_DEV + 1, PLANES, LANES), F32)] * 4,
        "gather",
        4,
    )(partners, pair_list, arrived, energy)
    return call(
        finish_kernel,
        [shape(*orbitals.shape), shape(ORB_DEV, dtype=F32)],
        [VMEM] * 3,
        [],
        "finish",
        3,
        out_specs=[VMEM, SMEM],
    )(to_all(due), total, energy)


def solution(mesh):
    return jax.shard_map(
        local,
        mesh=mesh,
        in_specs=(P("orb", "grid", None), P(None, "orb"), P()),
        out_specs=(P("orb", "grid", None), P("orb")),
        check_vma=False,
    )
```

```python
import functools

import jax
import jax.numpy as jnp
import ml_dtypes
import numpy as np
from jax import lax
from jax.experimental import pallas as pl
from jax.experimental.pallas import tpu as pltpu
from jax.sharding import PartitionSpec as P

BOX = 64
LANES = 128
TILES = BOX * BOX // LANES
PLANES = 8
ROWS = TILES * PLANES
GRID = 8
PAIRS = GRID // 2
ORDER = (2, 1, 3)
UP, DOWN, MIDDLE, CARRY, PAST_UP, PAST_DOWN = 0, 8, 16, 24, 27, 28
ORB_DEV = 8
ENTRIES = 16
HALF = ENTRIES // 2
PAD = 10
MU2 = 0.02
BF16 = jnp.bfloat16
F32 = jnp.float32
VMEM_LIMIT = 40 * 1024 * 1024


def sine64():
    steps = np.arange(1, BOX + 1, dtype=np.float64)
    return np.sqrt(2.0 / (BOX + 1)) * np.sin(np.pi * steps[:, None] * steps[None, :] / (BOX + 1))


def high_low(table):
    high = table.astype(np.float32).astype(ml_dtypes.bfloat16)
    rest = table - high.astype(np.float64)
    return high, rest.astype(np.float32).astype(ml_dtypes.bfloat16)


def sine_factors():
    sine = sine64()
    zero = np.zeros((BOX, BOX))
    high, low = high_low(np.block([[sine, zero], [zero, sine]]))
    y_right = np.concatenate(
        [np.concatenate([high, low], 1), np.concatenate([high, np.zeros_like(high)], 1)], 0
    )
    half = 2 * np.arange(TILES)
    rows = []
    for h in range(2):
        rows.append(np.concatenate([sine[np.ix_(half + h, half + h)], sine[np.ix_(half + h, half + 1 - h)]], 1))
    high, low = high_low(np.concatenate(rows, 0))
    return jnp.asarray(y_right), jnp.asarray(np.concatenate([high, high, low], 1))


def z_factors(grid_index):
    steps = jnp.arange(1, BOX + 1).astype(F32)
    eigen = 2.0 - 2.0 * jnp.cos(jnp.pi * steps / (BOX + 1))
    s = (eigen[:, None] + eigen[None, :] + MU2).reshape(TILES, LANES)[None]
    theta = jnp.log(1.0 + 0.5 * s + jnp.sqrt(s + 0.25 * s * s))

    def number(n):
        return jnp.asarray(n).reshape(-1).astype(F32)[:, None, None]

    def rest(n):
        return 1.0 - jnp.exp(-2.0 * theta * number(n))

    def fall(n):
        return jnp.exp(-theta * number(n))

    z = grid_index * PLANES + jnp.arange(PLANES)
    up = fall(1) * rest(z) / rest(z + 1)
    down = fall(1) * rest(63 - z) / rest(64 - z)
    scale = MU2 / (rest(1) * rest(65))
    middle = scale * fall(1) * rest(z + 1) * rest(64 - z)
    pair = grid_index // 2
    e = jnp.arange(1, PAIRS)
    other = (pair - e) % PAIRS
    below = e <= pair
    away = jnp.where(below, 8 * grid_index - 16 * other - 16, 16 * other - 8 * grid_index - 8)
    first = jnp.where(below, 16 * other + 16, 64 - 16 * other)
    last = jnp.where(below, 8 * grid_index, 56 - 8 * grid_index)
    carry = fall(away) * rest(first) / rest(last)
    edge = 16 * pair + 8
    past_up = fall(8) * rest(edge) / rest(edge + 8)
    past_down = fall(8) * rest(64 - edge) / rest(72 - edge)
    return jnp.concatenate([up, down, middle, carry, past_up, past_down], 0)


def lane_iota(rows):
    return lax.broadcasted_iota(jnp.int32, (rows, LANES), 1)


def split(value):
    high = value.astype(BF16)
    return high, (value - high.astype(F32)).astype(BF16)


def dot(left, right):
    return jnp.dot(left, right, preferred_element_type=F32)


def times_y(value, y_right):
    high, low = split(value)
    both = dot(jnp.concatenate([high, low], axis=1), y_right)
    return both[:, :LANES] + both[:, LANES:]


def times_x(planes, x_left, terms):
    value = jnp.concatenate(planes, axis=1)
    other = jnp.concatenate([pltpu.roll(p, BOX, 1) for p in planes], axis=1)
    data = jnp.concatenate([value, other], axis=0)
    if terms == 1:
        high = data.astype(BF16)
        both = dot(x_left[:, BOX:], jnp.concatenate([high, high], axis=0))
    else:
        high, low = split(data)
        both = dot(x_left, jnp.concatenate([high, low, high], axis=0))
    first = lane_iota(TILES) < BOX
    out = []
    for z in range(PLANES):
        tile = both[:, LANES * z : LANES * (z + 1)]
        out.append(jnp.where(first, tile[:TILES], tile[TILES:]))
    return out


def shifted(value, step_x, step_y, buffer):
    buffer[PAD * 8 : PAD * 8 + ROWS, :] = value
    flat = step_x * BOX + step_y
    tiles = flat >> 7
    lanes = flat & 127
    start = pl.multiple_of((tiles + PAD) * 8, 8)
    window = buffer[pl.ds(start, ROWS + 8), :]
    window = pltpu.roll(window, (LANES - lanes) & 127, 1)
    lane = lane_iota(ROWS)
    moved = jnp.where(lane < LANES - lanes, window[:ROWS], window[8:])
    y_new = (lane & (BOX - 1)) + step_y
    return jnp.where((y_new >= 0) & (y_new < BOX), moved, 0.0)


def clear_margins(buffer):
    zero = jnp.zeros((PAD * 8, LANES), F32)
    buffer[: PAD * 8, :] = zero
    buffer[PAD * 8 + ROWS :, :] = zero


def column_sums(value):
    return jnp.sum(value, axis=0, keepdims=True)


def forward(rho, tables, held, coeffs, ends, message, n):
    y_right, x_left, z_table = tables
    held[...] = times_y(rho, y_right[...])
    planes = times_x([held[pl.ds(z, TILES, stride=PLANES), :] for z in range(PLANES)], x_left[...], 1)
    for z in range(PLANES):
        coeffs[n, TILES * z : TILES * (z + 1), :] = planes[z]
    above = planes[0]
    for z in range(1, PLANES):
        above = z_table[UP + z] * above + planes[z]
    below = planes[PLANES - 1]
    for z in range(PLANES - 2, -1, -1):
        below = z_table[DOWN + z] * below + planes[z]
    both = jnp.concatenate([above, below], axis=0)
    ends[n] = both
    message[2 * TILES * n : 2 * TILES * (n + 1), :] = both.astype(BF16)


def halves(message, n):
    both = message[2 * TILES * n : 2 * TILES * (n + 1), :].astype(F32)
    return both[:TILES], both[TILES:]


def inverse(grid, near, sums, coeffs, tables, held, n):
    y_right, x_left, z_table = tables
    near_up, near_down = halves(near, n)
    upper = (grid & 1) == 1
    from_below = jnp.where(upper, near_up, 0.0)
    from_above = jnp.where(upper, 0.0, near_down)
    for e in range(1, PAIRS):
        below = e <= (grid >> 1)
        term = z_table[CARRY + e - 1] * sums[e - 1]
        from_below += jnp.where(below, term, 0.0)
        from_above += jnp.where(below, 0.0, term)
    planes = [coeffs[n, TILES * z : TILES * (z + 1), :] for z in range(PLANES)]
    ups = []
    for z in range(PLANES):
        from_below = z_table[UP + z] * from_below + planes[z]
        ups.append(from_below)
    solved = [None] * PLANES
    product = jnp.zeros((TILES, LANES), F32)
    for z in range(PLANES - 1, -1, -1):
        carried = z_table[DOWN + z] * from_above
        solved[z] = z_table[MIDDLE + z] * (ups[z] + carried)
        from_above = planes[z] + carried
        product += planes[z] * solved[z]
    full = times_y(jnp.concatenate(times_x(solved, x_left[...], 1), axis=0), y_right[...])
    for z in range(PLANES):
        held[pl.ds(z, TILES, stride=PLANES), :] = full[TILES * z : TILES * (z + 1)]
    return held[...], column_sums(product)


def pair_scalars(pairs, anchor, n):
    owner = pairs[0, n]
    mate = jnp.maximum(pairs[1, n], 0)
    step_x = anchor[0, owner] - anchor[0, mate]
    step_y = anchor[1, owner] - anchor[1, mate]
    return pairs[1, n] >= 0, owner & (ORB_DEV - 1), step_x, step_y


def tile(box, t):
    return box[PLANES * t : PLANES * (t + 1)]


def rows_kernel(orb, orb_rows):
    for n in range(ORB_DEV):
        wide = orb[n].astype(F32)
        box = jnp.concatenate([wide[:, LANES * t : LANES * (t + 1)] for t in range(TILES)], axis=0)
        orb_rows[n] = box.astype(BF16)


def spread_kernel(pairs, orb, out):
    wide = [orb[n].astype(F32) for n in range(ORB_DEV)]
    rows = lax.broadcasted_iota(jnp.int32, (ENTRIES, LANES), 0)
    partners = jnp.zeros((ENTRIES, LANES), F32)
    for n in range(ENTRIES):
        partners = jnp.where(rows == n, pairs[1, n].astype(F32), partners)
    partners = partners.astype(BF16)
    for t in range(TILES):
        piece = jnp.concatenate([w[:, LANES * t : LANES * (t + 1)] for w in wide], axis=0)
        out[t, : ORB_DEV * PLANES, :] = piece.astype(BF16)
        out[t, ORB_DEV * PLANES :, :] = partners


def serve_kernel(partners, held, out, every):
    count = held.shape[0]
    for d in range(count):
        pieces = held[d, : ORB_DEV * PLANES, :].astype(F32)
        for n in range(ORB_DEV):
            every[ORB_DEV * d + n] = tile(pieces, n)

    def step(i, carry):
        for d in range(4):
            d += 4 * i
            pieces = [every[jnp.maximum(partners[ENTRIES * d + n], 0)] for n in range(ENTRIES)]
            out[d] = jnp.concatenate(pieces, axis=0).astype(BF16)
        return carry

    lax.fori_loop(0, count // 4, step, 0)


def base_forward_kernel(orb_rows, y_right, x_left, z_table, coeffs, ends, message, *held):
    for n in range(ORB_DEV):
        box = orb_rows[n].astype(F32)
        forward(box * box, (y_right, x_left, z_table), held[n], coeffs, ends, message, n)


def pair_forward_kernel(start, pairs, anchor, orb_rows, fetched, y_right, x_left, z_table, moved_out, coeffs, ends, message, *refs):
    buffers, held = refs[:HALF], refs[HALF:]
    for n in range(HALF):
        clear_margins(buffers[n])
    for m in range(0, HALF, 2):
        row = PLANES * (start + m)
        both = [fetched[t, row : row + 2 * PLANES, :].astype(F32) for t in range(TILES)]
        for n in (m, m + 1):
            _, owner, step_x, step_y = pair_scalars(pairs, anchor, start + n)
            mate = jnp.concatenate([tile(b, n - m) for b in both], axis=0)
            moved = shifted(mate, step_x, step_y, buffers[n])
            moved_out[n] = moved.astype(BF16)
            rho = orb_rows[owner].astype(F32) * moved
            forward(rho, (y_right, x_left, z_table), held[n], coeffs, ends, message, n)


def pair_up_kernel(grid, ends, near, z_table, *outs):
    pair, upper = grid[0] >> 1, (grid[0] & 1) == 1
    for n in range(ends.shape[0]):
        near_up, near_down = halves(near, n)
        mine = ends[n]
        mine_up, mine_down = mine[:TILES], mine[TILES:]
        low_up = jnp.where(upper, near_up, mine_up)
        high_up = jnp.where(upper, mine_up, near_up)
        low_down = jnp.where(upper, near_down, mine_down)
        high_down = jnp.where(upper, mine_down, near_down)
        up = (z_table[PAST_UP] * low_up + high_up).astype(BF16)
        down = (low_down + z_table[PAST_DOWN] * high_down).astype(BF16)
        for e in range(1, PAIRS):
            outs[e - 1][n] = jnp.where(pair + e < PAIRS, up, down)


def in_order(refs, n):
    return [refs[ORDER.index(e)][n].astype(F32) for e in range(1, PAIRS)]


def base_inverse_kernel(grid, near, *refs):
    sums, refs = refs[: PAIRS - 1], refs[PAIRS - 1 :]
    coeffs, orb_rows, y_right, x_left, z_table, total, energy, *held = refs
    tables = (y_right, x_left, z_table)
    for n in range(ORB_DEV):
        potential, value = inverse(grid[0], near, in_order(sums, n), coeffs, tables, held[n], n)
        total[n] = orb_rows[n].astype(F32) * potential
        energy[n : n + 1, :] = value


def pair_inverse_kernel(start, grid, pairs, anchor, near, *refs):
    sums, refs = refs[: PAIRS - 1], refs[PAIRS - 1 :]
    coeffs, orb_rows, moved, y_right, x_left, z_table, total_in, out_in, total, out, energy, *refs = refs
    buffers, held = refs[:HALF], refs[HALF:]
    tables = (y_right, x_left, z_table)
    for n in range(HALF):
        clear_margins(buffers[n])
    total[...] = total_in[...]
    if start:
        out[:, : PLANES * start, :] = out_in[:, : PLANES * start, :]
    for m in range(0, HALF, 2):
        backs = []
        for n in (m, m + 1):
            _, owner, step_x, step_y = pair_scalars(pairs, anchor, start + n)
            potential, value = inverse(grid[0], near, in_order(sums, n), coeffs, tables, held[n], n)
            energy[n : n + 1, :] = value
            backs.append(shifted(orb_rows[owner].astype(F32) * potential, -step_x, -step_y, buffers[n]))
        row = PLANES * (start + m)
        for t in range(TILES):
            piece = jnp.concatenate([tile(back, t) for back in backs], axis=0)
            out[t, row : row + 2 * PLANES, :] = piece.astype(BF16)
    for n in range(HALF):
        live, owner, _, _ = pair_scalars(pairs, anchor, start + n)
        total[owner] += jnp.where(live, moved[n].astype(F32) * held[n][...], 0.0)


def gather_kernel(partners, pairs, arrived, energy, out, energy_here, every_energy, *every):
    count = arrived.shape[0]
    spare = ORB_DEV * count
    for part in every:
        part[...] = jnp.zeros_like(part)

    def step(i, carry):
        for d in (2 * i, 2 * i + 1):
            for m in range(0, ENTRIES, 2):
                both = arrived[d, PLANES * m : PLANES * (m + 2), :].astype(F32)
                for n in (m, m + 1):
                    which = partners[ENTRIES * d + n]
                    which = jnp.where(which >= 0, which, spare)
                    every[n % len(every)][which] += tile(both, n - m)
        return carry

    lax.fori_loop(0, count // 2, step, 0)
    every_energy[...] = jnp.zeros_like(every_energy)
    first = lane_iota(1) == 0
    for n in range(ORB_DEV):
        energy_here[n : n + 1, :] = jnp.where(first, energy[n], 0.0)
    for n in range(ENTRIES):
        mate = pairs[1, n]
        owner = pairs[0, n] & (ORB_DEV - 1)
        value = jnp.where(first & (mate >= 0), energy[ORB_DEV + n], 0.0)
        every_energy[pl.ds(jnp.where(mate >= 0, mate, spare), 1), :] += value
        energy_here[pl.ds(owner, 1), :] += value
    for d in range(count):
        pieces = [sum(part[ORB_DEV * d + n] for part in every) for n in range(ORB_DEV)]
        out[d, : ORB_DEV * PLANES, :] = jnp.concatenate(pieces, axis=0).astype(BF16)
        value = every_energy[ORB_DEV * d : ORB_DEV * (d + 1), :]
        high = value.astype(BF16).astype(F32)
        out[d, ORB_DEV * PLANES :, :] = jnp.concatenate([high, value - high], axis=0).astype(BF16)


def finish_kernel(arrived, total, energy, out, energy_out):
    sums = energy[...]
    for t in range(TILES):
        pieces = arrived[t, : ORB_DEV * PLANES, :].astype(F32)
        for n in range(ORB_DEV):
            here = total[n, PLANES * t : PLANES * (t + 1), :] + tile(pieces, n)
            out[n, :, LANES * t : LANES * (t + 1)] = here.astype(BF16)
        both = arrived[t, ORB_DEV * PLANES :, :].astype(F32)
        sums += both[:ORB_DEV] + both[ORB_DEV:]
    for n in range(ORB_DEV):
        energy_out[n] = jnp.sum(sums[n : n + 1, :])


VMEM = pl.BlockSpec(memory_space=pltpu.VMEM)
SMEM = pl.BlockSpec(memory_space=pltpu.SMEM)
ANY = pl.BlockSpec(memory_space=pl.ANY)
HELD = pltpu.VMEM((ROWS, LANES), F32)
SHIFT_BUFFER = pltpu.VMEM(((2 * PAD + TILES) * 8, LANES), F32)


def shape(*dims, dtype=BF16):
    return jax.ShapeDtypeStruct(dims, dtype)


def solve_shapes(count):
    return [
        shape(count, ROWS, LANES, dtype=F32),
        shape(count, 2 * TILES, LANES, dtype=F32),
        shape(count * 2 * TILES, LANES),
    ]


def call(kernel, out_shape, in_specs, scratch, name, micros, out_specs=None, aliases=None):
    return pl.pallas_call(
        kernel,
        out_shape=out_shape,
        in_specs=in_specs,
        out_specs=out_specs if out_specs is not None else jax.tree.map(lambda _: VMEM, out_shape),
        scratch_shapes=scratch,
        input_output_aliases=aliases or {},
        name=name,
        cost_estimate=pl.CostEstimate(flops=0, bytes_accessed=int(micros * 3.0e6), transcendentals=0),
        compiler_params=pltpu.CompilerParams(vmem_limit_bytes=VMEM_LIMIT),
    )


def local(orbitals, pair_list, box_anchor):
    devices = lax.axis_size("orb")
    grid_index = lax.axis_index("grid")
    grid = grid_index.astype(jnp.int32).reshape(1)
    y_right, x_left = sine_factors()
    z_table = z_factors(grid_index)
    tables = (y_right, x_left, z_table)
    spread = ORB_DEV * PLANES + ENTRIES
    totals = shape(ORB_DEV, ROWS, LANES, dtype=F32)

    def to_all(blocks):
        return lax.all_to_all(blocks, "orb", split_axis=0, concat_axis=0, tiled=True)

    def to_near(message):
        return lax.ppermute(message, "grid", [(i, i ^ 1) for i in range(GRID)])

    def from_pairs(ends, near):
        outs = [shape(ends.shape[0], TILES, LANES)] * (PAIRS - 1)
        sums = call(pair_up_kernel, outs, [SMEM] + [VMEM] * 3, [], "pair_up", 1)(grid, ends, near, z_table)
        hops = [[(i, (i + 2 * e) % GRID) for i in range(GRID)] for e in ORDER]
        return [lax.ppermute(sums[e - 1], "grid", hop) for e, hop in zip(ORDER, hops)]

    pieces = call(spread_kernel, shape(devices, spread, LANES), [SMEM, VMEM], [], "spread", 1)(
        pair_list, orbitals
    )
    orbitals, _ = lax.optimization_barrier((orbitals, pieces))
    orb_rows = call(rows_kernel, shape(ORB_DEV, ROWS, LANES), [VMEM], [], "rows", 1)(orbitals)
    pieces = to_all(pieces)
    base_coeffs, base_ends, message = call(
        base_forward_kernel, solve_shapes(ORB_DEV), [VMEM] * 4, [HELD] * ORB_DEV, "base_forward", 2
    )(orb_rows, *tables)
    pieces, base_near = lax.optimization_barrier((pieces, to_near(message)))
    partners = pieces[:, ORB_DEV * PLANES :, 0].astype(jnp.int32).reshape(-1)
    served = call(
        serve_kernel,
        shape(devices, ENTRIES * PLANES, LANES),
        [SMEM, VMEM],
        [pltpu.VMEM((devices * ORB_DEV, PLANES, LANES), F32)],
        "serve",
        2,
    )(partners, pieces)
    fetched = to_all(served)
    base_sums = from_pairs(base_ends, base_near)
    fetched, base_sums = lax.optimization_barrier((fetched, base_sums))
    total, base_energy = call(
        base_inverse_kernel,
        [totals, shape(ORB_DEV, LANES, dtype=F32)],
        [SMEM] + [VMEM] * (PAIRS + 5),
        [HELD] * ORB_DEV,
        "base_inverse",
        2,
    )(grid, base_near, *base_sums, base_coeffs, orb_rows, *tables)

    parts = []
    for start in range(0, ENTRIES, HALF):
        moved, coeffs, ends, message = call(
            functools.partial(pair_forward_kernel, start),
            [shape(HALF, ROWS, LANES)] + solve_shapes(HALF),
            [SMEM] * 2 + [VMEM] * 5,
            [SHIFT_BUFFER] * HALF + [HELD] * HALF,
            "pair_forward",
            2,
        )(pair_list, box_anchor, orb_rows, fetched, *tables)
        parts.append((start, moved, coeffs, ends, to_near(message)))
    start, moved, coeffs, ends, near = parts[0]
    total, near = lax.optimization_barrier((total, near))
    parts[0] = (start, moved, coeffs, ends, near)
    parts = [(*part, from_pairs(part[3], part[4])) for part in parts]
    back, energy = served, [base_energy]
    for start, moved, coeffs, ends, near, sums in parts:
        total, back, value = call(
            functools.partial(pair_inverse_kernel, start),
            [totals, shape(devices, ENTRIES * PLANES, LANES), shape(HALF, LANES, dtype=F32)],
            [SMEM] * 3 + [VMEM] * (PAIRS + 7) + [VMEM if start else ANY],
            [SHIFT_BUFFER] * HALF + [HELD] * HALF,
            "pair_inverse",
            3,
            aliases={PAIRS + 9: 0, PAIRS + 10: 1} if start else {PAIRS + 9: 0},
        )(grid, pair_list, box_anchor, near, *sums, coeffs, orb_rows, moved, *tables, total, back)
        energy.append(value)

    arrived = to_all(back)
    energy = lax.psum(jnp.sum(jnp.concatenate(energy), axis=1), "grid")
    due, energy = call(
        gather_kernel,
        [shape(devices, spread, LANES), shape(ORB_DEV, LANES, dtype=F32)],
        [SMEM] * 2 + [VMEM, SMEM],
        [pltpu.VMEM((devices * ORB_DEV + 8, LANES), F32)]
        + [pltpu.VMEM((devices * ORB_DEV + 1, PLANES, LANES), F32)] * 4,
        "gather",
        4,
    )(partners, pair_list, arrived, energy)
    return call(
        finish_kernel,
        [shape(*orbitals.shape), shape(ORB_DEV, dtype=F32)],
        [VMEM] * 3,
        [],
        "finish",
        3,
        out_specs=[VMEM, SMEM],
    )(to_all(due), total, energy)


def solution(mesh):
    return jax.shard_map(
        local,
        mesh=mesh,
        in_specs=(P("orb", "grid", None), P(None, "orb"), P()),
        out_specs=(P("orb", "grid", None), P("orb")),
        check_vma=False,
    )
```

```python
import functools

import jax
import jax.numpy as jnp
import ml_dtypes
import numpy as np
from jax import lax
from jax.experimental import pallas as pl
from jax.experimental.pallas import tpu as pltpu
from jax.sharding import PartitionSpec as P

BOX = 64
LANES = 128
TILES = BOX * BOX // LANES
PLANES = 8
ROWS = TILES * PLANES
GRID = 8
PAIRS = GRID // 2
ORDER = (2, 1, 3)
UP, DOWN, MIDDLE, CARRY, PAST_UP, PAST_DOWN = 0, 8, 16, 24, 27, 28
ORB_DEV = 8
ENTRIES = 16
EXTRA = 8
HALF = ENTRIES // 2
PAD = 10
MU2 = 0.02
BF16 = jnp.bfloat16
F32 = jnp.float32
VMEM_LIMIT = 40 * 1024 * 1024


def sine64():
    steps = np.arange(1, BOX + 1, dtype=np.float64)
    return np.sqrt(2.0 / (BOX + 1)) * np.sin(np.pi * steps[:, None] * steps[None, :] / (BOX + 1))


def high_low(table):
    high = table.astype(np.float32).astype(ml_dtypes.bfloat16)
    rest = table - high.astype(np.float64)
    return high, rest.astype(np.float32).astype(ml_dtypes.bfloat16)


def sine_factors():
    sine = sine64()
    zero = np.zeros((BOX, BOX))
    high, low = high_low(np.block([[sine, zero], [zero, sine]]))
    y_right = np.concatenate(
        [np.concatenate([high, low], 1), np.concatenate([high, np.zeros_like(high)], 1)], 0
    )
    half = 2 * np.arange(TILES)
    rows = []
    for h in range(2):
        rows.append(np.concatenate([sine[np.ix_(half + h, half + h)], sine[np.ix_(half + h, half + 1 - h)]], 1))
    high, low = high_low(np.concatenate(rows, 0))
    return jnp.asarray(y_right), jnp.asarray(np.concatenate([high, high, low], 1))


def z_factors(grid_index):
    steps = jnp.arange(1, BOX + 1).astype(F32)
    eigen = 2.0 - 2.0 * jnp.cos(jnp.pi * steps / (BOX + 1))
    s = (eigen[:, None] + eigen[None, :] + MU2).reshape(TILES, LANES)[None]
    theta = jnp.log(1.0 + 0.5 * s + jnp.sqrt(s + 0.25 * s * s))

    def number(n):
        return jnp.asarray(n).reshape(-1).astype(F32)[:, None, None]

    def rest(n):
        return 1.0 - jnp.exp(-2.0 * theta * number(n))

    def fall(n):
        return jnp.exp(-theta * number(n))

    z = grid_index * PLANES + jnp.arange(PLANES)
    up = fall(1) * rest(z) / rest(z + 1)
    down = fall(1) * rest(63 - z) / rest(64 - z)
    scale = MU2 / (rest(1) * rest(65))
    middle = scale * fall(1) * rest(z + 1) * rest(64 - z)
    pair = grid_index // 2
    e = jnp.arange(1, PAIRS)
    other = (pair - e) % PAIRS
    below = e <= pair
    away = jnp.where(below, 8 * grid_index - 16 * other - 16, 16 * other - 8 * grid_index - 8)
    first = jnp.where(below, 16 * other + 16, 64 - 16 * other)
    last = jnp.where(below, 8 * grid_index, 56 - 8 * grid_index)
    carry = fall(away) * rest(first) / rest(last)
    edge = 16 * pair + 8
    past_up = fall(8) * rest(edge) / rest(edge + 8)
    past_down = fall(8) * rest(64 - edge) / rest(72 - edge)
    return jnp.concatenate([up, down, middle, carry, past_up, past_down], 0)


def lane_iota(rows):
    return lax.broadcasted_iota(jnp.int32, (rows, LANES), 1)


def split(value):
    high = value.astype(BF16)
    return high, (value - high.astype(F32)).astype(BF16)


def dot(left, right):
    return jnp.dot(left, right, preferred_element_type=F32)


def times_y(value, y_right):
    high, low = split(value)
    both = dot(jnp.concatenate([high, low], axis=1), y_right)
    return both[:, :LANES] + both[:, LANES:]


def times_x(planes, x_left, terms):
    value = jnp.concatenate(planes, axis=1)
    other = jnp.concatenate([pltpu.roll(p, BOX, 1) for p in planes], axis=1)
    data = jnp.concatenate([value, other], axis=0)
    if terms == 1:
        high = data.astype(BF16)
        both = dot(x_left[:, BOX:], jnp.concatenate([high, high], axis=0))
    else:
        high, low = split(data)
        both = dot(x_left, jnp.concatenate([high, low, high], axis=0))
    first = lane_iota(TILES) < BOX
    out = []
    for z in range(PLANES):
        tile = both[:, LANES * z : LANES * (z + 1)]
        out.append(jnp.where(first, tile[:TILES], tile[TILES:]))
    return out


def shifted(value, step_x, step_y, buffer):
    buffer[PAD * 8 : PAD * 8 + ROWS, :] = value
    flat = step_x * BOX + step_y
    tiles = flat >> 7
    lanes = flat & 127
    start = pl.multiple_of((tiles + PAD) * 8, 8)
    window = buffer[pl.ds(start, ROWS + 8), :]
    window = pltpu.roll(window, (LANES - lanes) & 127, 1)
    lane = lane_iota(ROWS)
    moved = jnp.where(lane < LANES - lanes, window[:ROWS], window[8:])
    y_new = (lane & (BOX - 1)) + step_y
    return jnp.where((y_new >= 0) & (y_new < BOX), moved, 0.0)


def clear_margins(buffer):
    zero = jnp.zeros((PAD * 8, LANES), F32)
    buffer[: PAD * 8, :] = zero
    buffer[PAD * 8 + ROWS :, :] = zero


def column_sums(value):
    return jnp.sum(value, axis=0, keepdims=True)


def forward(rho, tables, held, coeffs, ends, message, n):
    y_right, x_left, z_table = tables
    held[...] = times_y(rho, y_right[...])
    planes = times_x([held[pl.ds(z, TILES, stride=PLANES), :] for z in range(PLANES)], x_left[...], 1)
    for z in range(PLANES):
        coeffs[n, TILES * z : TILES * (z + 1), :] = planes[z]
    above = planes[0]
    for z in range(1, PLANES):
        above = z_table[UP + z] * above + planes[z]
    below = planes[PLANES - 1]
    for z in range(PLANES - 2, -1, -1):
        below = z_table[DOWN + z] * below + planes[z]
    both = jnp.concatenate([above, below], axis=0)
    ends[n] = both
    message[2 * TILES * n : 2 * TILES * (n + 1), :] = both.astype(BF16)


def halves(message, n):
    both = message[2 * TILES * n : 2 * TILES * (n + 1), :].astype(F32)
    return both[:TILES], both[TILES:]


def inverse(grid, near, sums, coeffs, tables, held, n):
    y_right, x_left, z_table = tables
    near_up, near_down = halves(near, n)
    upper = (grid & 1) == 1
    from_below = jnp.where(upper, near_up, 0.0)
    from_above = jnp.where(upper, 0.0, near_down)
    for e in range(1, PAIRS):
        below = e <= (grid >> 1)
        term = z_table[CARRY + e - 1] * sums[e - 1]
        from_below += jnp.where(below, term, 0.0)
        from_above += jnp.where(below, 0.0, term)
    planes = [coeffs[n, TILES * z : TILES * (z + 1), :] for z in range(PLANES)]
    ups = []
    for z in range(PLANES):
        from_below = z_table[UP + z] * from_below + planes[z]
        ups.append(from_below)
    solved = [None] * PLANES
    product = jnp.zeros((TILES, LANES), F32)
    for z in range(PLANES - 1, -1, -1):
        carried = z_table[DOWN + z] * from_above
        solved[z] = z_table[MIDDLE + z] * (ups[z] + carried)
        from_above = planes[z] + carried
        product += planes[z] * solved[z]
    full = times_y(jnp.concatenate(times_x(solved, x_left[...], 1), axis=0), y_right[...])
    for z in range(PLANES):
        held[pl.ds(z, TILES, stride=PLANES), :] = full[TILES * z : TILES * (z + 1)]
    return held[...], column_sums(product)


def pair_scalars(pairs, anchor, n):
    owner = pairs[0, n]
    mate = jnp.maximum(pairs[1, n], 0)
    step_x = anchor[0, owner] - anchor[0, mate]
    step_y = anchor[1, owner] - anchor[1, mate]
    return pairs[1, n] >= 0, owner & (ORB_DEV - 1), step_x, step_y


def tile(box, t):
    return box[PLANES * t : PLANES * (t + 1)]


def rows_kernel(orb, orb_rows):
    for n in range(ORB_DEV):
        wide = orb[n].astype(F32)
        box = jnp.concatenate([wide[:, LANES * t : LANES * (t + 1)] for t in range(TILES)], axis=0)
        orb_rows[n] = box.astype(BF16)


def spread_kernel(pairs, orb, out):
    wide = [orb[n].astype(F32) for n in range(ORB_DEV)]
    place = lax.broadcasted_iota(jnp.int32, (EXTRA, LANES), 0) * 2 + lane_iota(EXTRA)
    partners = jnp.zeros((EXTRA, LANES), F32)
    for n in range(ENTRIES):
        here = (place == n) & (lane_iota(EXTRA) < 2)
        partners = jnp.where(here, pairs[1, n].astype(F32), partners)
    partners = partners.astype(BF16)
    for t in range(TILES):
        piece = jnp.concatenate([w[:, LANES * t : LANES * (t + 1)] for w in wide], axis=0)
        out[t, : ORB_DEV * PLANES, :] = piece.astype(BF16)
        out[t, ORB_DEV * PLANES :, :] = partners


def serve_kernel(partners, held, out, every):
    count = held.shape[0]
    for d in range(count):
        pieces = held[d, : ORB_DEV * PLANES, :].astype(F32)
        for n in range(ORB_DEV):
            every[ORB_DEV * d + n] = tile(pieces, n)

    def step(i, carry):
        for d in range(4):
            d += 4 * i
            pieces = [every[jnp.maximum(partners[ENTRIES * d + n], 0)] for n in range(ENTRIES)]
            out[d] = jnp.concatenate(pieces, axis=0).astype(BF16)
        return carry

    lax.fori_loop(0, count // 4, step, 0)


def base_forward_kernel(orb_rows, y_right, x_left, z_table, coeffs, ends, message, *held):
    for n in range(ORB_DEV):
        box = orb_rows[n].astype(F32)
        forward(box * box, (y_right, x_left, z_table), held[n], coeffs, ends, message, n)


def pair_forward_kernel(start, pairs, anchor, orb_rows, fetched, y_right, x_left, z_table, moved_out, coeffs, ends, message, *refs):
    buffers, held = refs[:HALF], refs[HALF:]
    for n in range(HALF):
        clear_margins(buffers[n])
    for m in range(0, HALF, 2):
        row = PLANES * (start + m)
        both = [fetched[t, row : row + 2 * PLANES, :].astype(F32) for t in range(TILES)]
        for n in (m, m + 1):
            _, owner, step_x, step_y = pair_scalars(pairs, anchor, start + n)
            mate = jnp.concatenate([tile(b, n - m) for b in both], axis=0)
            moved = shifted(mate, step_x, step_y, buffers[n])
            moved_out[n] = moved.astype(BF16)
            rho = orb_rows[owner].astype(F32) * moved
            forward(rho, (y_right, x_left, z_table), held[n], coeffs, ends, message, n)


def pair_up_kernel(grid, ends, near, z_table, *outs):
    pair, upper = grid[0] >> 1, (grid[0] & 1) == 1
    for n in range(ends.shape[0]):
        near_up, near_down = halves(near, n)
        mine = ends[n]
        mine_up, mine_down = mine[:TILES], mine[TILES:]
        low_up = jnp.where(upper, near_up, mine_up)
        high_up = jnp.where(upper, mine_up, near_up)
        low_down = jnp.where(upper, near_down, mine_down)
        high_down = jnp.where(upper, mine_down, near_down)
        up = (z_table[PAST_UP] * low_up + high_up).astype(BF16)
        down = (low_down + z_table[PAST_DOWN] * high_down).astype(BF16)
        for e in range(1, PAIRS):
            outs[e - 1][n] = jnp.where(pair + e < PAIRS, up, down)


def in_order(refs, n):
    return [refs[ORDER.index(e)][n].astype(F32) for e in range(1, PAIRS)]


def base_inverse_kernel(grid, near, *refs):
    sums, refs = refs[: PAIRS - 1], refs[PAIRS - 1 :]
    coeffs, orb_rows, y_right, x_left, z_table, total, energy, *held = refs
    tables = (y_right, x_left, z_table)
    for n in range(ORB_DEV):
        potential, value = inverse(grid[0], near, in_order(sums, n), coeffs, tables, held[n], n)
        total[n] = orb_rows[n].astype(F32) * potential
        energy[n : n + 1, :] = value


def pair_inverse_kernel(start, grid, pairs, anchor, near, *refs):
    sums, refs = refs[: PAIRS - 1], refs[PAIRS - 1 :]
    coeffs, orb_rows, moved, y_right, x_left, z_table, total_in, out_in, total, out, energy, *refs = refs
    buffers, held = refs[:HALF], refs[HALF:]
    tables = (y_right, x_left, z_table)
    for n in range(HALF):
        clear_margins(buffers[n])
    total[...] = total_in[...]
    if start:
        out[:, : PLANES * start, :] = out_in[:, : PLANES * start, :]
    for m in range(0, HALF, 2):
        backs = []
        for n in (m, m + 1):
            _, owner, step_x, step_y = pair_scalars(pairs, anchor, start + n)
            potential, value = inverse(grid[0], near, in_order(sums, n), coeffs, tables, held[n], n)
            energy[n : n + 1, :] = value
            backs.append(shifted(orb_rows[owner].astype(F32) * potential, -step_x, -step_y, buffers[n]))
        row = PLANES * (start + m)
        for t in range(TILES):
            piece = jnp.concatenate([tile(back, t) for back in backs], axis=0)
            out[t, row : row + 2 * PLANES, :] = piece.astype(BF16)
    for n in range(HALF):
        live, owner, _, _ = pair_scalars(pairs, anchor, start + n)
        total[owner] += jnp.where(live, moved[n].astype(F32) * held[n][...], 0.0)


def gather_kernel(partners, pairs, arrived, energy, out, energy_here, every_energy, *every):
    count = arrived.shape[0]
    spare = ORB_DEV * count
    for part in every:
        part[...] = jnp.zeros_like(part)

    def step(i, carry):
        for d in (2 * i, 2 * i + 1):
            for m in range(0, ENTRIES, 2):
                both = arrived[d, PLANES * m : PLANES * (m + 2), :].astype(F32)
                for n in (m, m + 1):
                    which = partners[ENTRIES * d + n]
                    which = jnp.where(which >= 0, which, spare)
                    every[n % len(every)][which] += tile(both, n - m)
        return carry

    lax.fori_loop(0, count // 2, step, 0)
    every_energy[...] = jnp.zeros_like(every_energy)
    first = lane_iota(1) == 0
    for n in range(ORB_DEV):
        energy_here[n : n + 1, :] = jnp.where(first, energy[n], 0.0)
    for n in range(ENTRIES):
        mate = pairs[1, n]
        owner = pairs[0, n] & (ORB_DEV - 1)
        value = jnp.where(first & (mate >= 0), energy[ORB_DEV + n], 0.0)
        every_energy[pl.ds(jnp.where(mate >= 0, mate, spare), 1), :] += value
        energy_here[pl.ds(owner, 1), :] += value
    for d in range(count):
        pieces = [sum(part[ORB_DEV * d + n] for part in every) for n in range(ORB_DEV)]
        out[d, : ORB_DEV * PLANES, :] = jnp.concatenate(pieces, axis=0).astype(BF16)
        value = every_energy[ORB_DEV * d : ORB_DEV * (d + 1), :]
        high = value.astype(BF16).astype(F32)
        low = pltpu.roll(value - high, 1, 1)
        out[d, ORB_DEV * PLANES :, :] = jnp.where(lane_iota(ORB_DEV) == 1, low, high).astype(BF16)


def finish_kernel(arrived, total, energy, out, energy_out):
    sums = energy[...]
    for t in range(TILES):
        pieces = arrived[t, : ORB_DEV * PLANES, :].astype(F32)
        for n in range(ORB_DEV):
            here = total[n, PLANES * t : PLANES * (t + 1), :] + tile(pieces, n)
            out[n, :, LANES * t : LANES * (t + 1)] = here.astype(BF16)
        sums += arrived[t, ORB_DEV * PLANES :, :].astype(F32)
    for n in range(ORB_DEV):
        energy_out[n] = jnp.sum(sums[n : n + 1, :])


VMEM = pl.BlockSpec(memory_space=pltpu.VMEM)
SMEM = pl.BlockSpec(memory_space=pltpu.SMEM)
ANY = pl.BlockSpec(memory_space=pl.ANY)
HELD = pltpu.VMEM((ROWS, LANES), F32)
SHIFT_BUFFER = pltpu.VMEM(((2 * PAD + TILES) * 8, LANES), F32)


def shape(*dims, dtype=BF16):
    return jax.ShapeDtypeStruct(dims, dtype)


def solve_shapes(count):
    return [
        shape(count, ROWS, LANES, dtype=F32),
        shape(count, 2 * TILES, LANES, dtype=F32),
        shape(count * 2 * TILES, LANES),
    ]


def call(kernel, out_shape, in_specs, scratch, name, micros, out_specs=None, aliases=None, limit=VMEM_LIMIT):
    return pl.pallas_call(
        kernel,
        out_shape=out_shape,
        in_specs=in_specs,
        out_specs=out_specs if out_specs is not None else jax.tree.map(lambda _: VMEM, out_shape),
        scratch_shapes=scratch,
        input_output_aliases=aliases or {},
        name=name,
        cost_estimate=pl.CostEstimate(flops=0, bytes_accessed=int(micros * 3.0e6), transcendentals=0),
        compiler_params=pltpu.CompilerParams(vmem_limit_bytes=limit),
    )


def local(orbitals, pair_list, box_anchor):
    devices = lax.axis_size("orb")
    grid_index = lax.axis_index("grid")
    grid = grid_index.astype(jnp.int32).reshape(1)
    y_right, x_left = sine_factors()
    z_table = z_factors(grid_index)
    tables = (y_right, x_left, z_table)
    spread = ORB_DEV * PLANES + EXTRA
    totals = shape(ORB_DEV, ROWS, LANES, dtype=F32)

    def to_all(blocks):
        return lax.all_to_all(blocks, "orb", split_axis=0, concat_axis=0, tiled=True)

    def to_near(message):
        return lax.ppermute(message, "grid", [(i, i ^ 1) for i in range(GRID)])

    def from_pairs(ends, near):
        outs = [shape(ends.shape[0], TILES, LANES)] * (PAIRS - 1)
        sums = call(pair_up_kernel, outs, [SMEM] + [VMEM] * 3, [], "pair_up", 1)(grid, ends, near, z_table)
        hops = [[(i, (i + 2 * e) % GRID) for i in range(GRID)] for e in ORDER]
        return [lax.ppermute(sums[e - 1], "grid", hop) for e, hop in zip(ORDER, hops)]

    pieces = call(
        spread_kernel, shape(devices, spread, LANES), [SMEM, VMEM], [], "spread", 1, limit=62 * 1024 * 1024
    )(pair_list, orbitals)
    orbitals, _ = lax.optimization_barrier((orbitals, pieces))
    orb_rows = call(rows_kernel, shape(ORB_DEV, ROWS, LANES), [VMEM], [], "rows", 1)(orbitals)
    pieces = to_all(pieces)
    base_coeffs, base_ends, message = call(
        base_forward_kernel, solve_shapes(ORB_DEV), [VMEM] * 4, [HELD] * ORB_DEV, "base_forward", 2
    )(orb_rows, *tables)
    pieces, base_near = lax.optimization_barrier((pieces, to_near(message)))
    partners = pieces[:, ORB_DEV * PLANES :, :2].astype(jnp.int32).reshape(-1)
    served = call(
        serve_kernel,
        shape(devices, ENTRIES * PLANES, LANES),
        [SMEM, VMEM],
        [pltpu.VMEM((devices * ORB_DEV, PLANES, LANES), F32)],
        "serve",
        2,
    )(partners, pieces)
    fetched = to_all(served)
    base_sums = from_pairs(base_ends, base_near)
    fetched, base_sums = lax.optimization_barrier((fetched, base_sums))
    total, base_energy = call(
        base_inverse_kernel,
        [totals, shape(ORB_DEV, LANES, dtype=F32)],
        [SMEM] + [VMEM] * (PAIRS + 5),
        [HELD] * ORB_DEV,
        "base_inverse",
        2,
    )(grid, base_near, *base_sums, base_coeffs, orb_rows, *tables)

    parts = []
    for start in range(0, ENTRIES, HALF):
        moved, coeffs, ends, message = call(
            functools.partial(pair_forward_kernel, start),
            [shape(HALF, ROWS, LANES)] + solve_shapes(HALF),
            [SMEM] * 2 + [VMEM] * 5,
            [SHIFT_BUFFER] * HALF + [HELD] * HALF,
            "pair_forward",
            2,
        )(pair_list, box_anchor, orb_rows, fetched, *tables)
        parts.append((start, moved, coeffs, ends, to_near(message)))
    start, moved, coeffs, ends, near = parts[0]
    total, near = lax.optimization_barrier((total, near))
    parts[0] = (start, moved, coeffs, ends, near)
    parts = [(*part, from_pairs(part[3], part[4])) for part in parts]
    back, energy = served, [base_energy]
    for start, moved, coeffs, ends, near, sums in parts:
        total, back, value = call(
            functools.partial(pair_inverse_kernel, start),
            [totals, shape(devices, ENTRIES * PLANES, LANES), shape(HALF, LANES, dtype=F32)],
            [SMEM] * 3 + [VMEM] * (PAIRS + 7) + [VMEM if start else ANY],
            [SHIFT_BUFFER] * HALF + [HELD] * HALF,
            "pair_inverse",
            3,
            aliases={PAIRS + 9: 0, PAIRS + 10: 1} if start else {PAIRS + 9: 0},
        )(grid, pair_list, box_anchor, near, *sums, coeffs, orb_rows, moved, *tables, total, back)
        energy.append(value)

    arrived = to_all(back)
    energy = lax.psum(jnp.sum(jnp.concatenate(energy), axis=1), "grid")
    due, energy = call(
        gather_kernel,
        [shape(devices, spread, LANES), shape(ORB_DEV, LANES, dtype=F32)],
        [SMEM] * 2 + [VMEM, SMEM],
        [pltpu.VMEM((devices * ORB_DEV + 8, LANES), F32)]
        + [pltpu.VMEM((devices * ORB_DEV + 1, PLANES, LANES), F32)] * 4,
        "gather",
        4,
    )(partners, pair_list, arrived, energy)
    return call(
        finish_kernel,
        [shape(*orbitals.shape), shape(ORB_DEV, dtype=F32)],
        [VMEM] * 3,
        [],
        "finish",
        3,
        out_specs=[VMEM, SMEM],
    )(to_all(due), total, energy)


def solution(mesh):
    return jax.shard_map(
        local,
        mesh=mesh,
        in_specs=(P("orb", "grid", None), P(None, "orb"), P()),
        out_specs=(P("orb", "grid", None), P("orb")),
        check_vma=False,
    )
```

```python
import functools

import jax
import jax.numpy as jnp
import ml_dtypes
import numpy as np
from jax import lax
from jax.experimental import pallas as pl
from jax.experimental.pallas import tpu as pltpu
from jax.sharding import PartitionSpec as P

BOX = 64
LANES = 128
TILES = BOX * BOX // LANES
PLANES = 8
ROWS = TILES * PLANES
GRID = 8
PAIRS = GRID // 2
ORDER = (2, 1, 3)
UP, DOWN, MIDDLE, CARRY, PAST_UP, PAST_DOWN = 0, 8, 16, 24, 27, 28
ORB_DEV = 8
ENTRIES = 16
EXTRA = 8
PARTS = ((0, 8), (8, 8))
PAD = 10
MU2 = 0.02
BF16 = jnp.bfloat16
F32 = jnp.float32
VMEM_LIMIT = 40 * 1024 * 1024


def sine64():
    steps = np.arange(1, BOX + 1, dtype=np.float64)
    return np.sqrt(2.0 / (BOX + 1)) * np.sin(np.pi * steps[:, None] * steps[None, :] / (BOX + 1))


def high_low(table):
    high = table.astype(np.float32).astype(ml_dtypes.bfloat16)
    rest = table - high.astype(np.float64)
    return high, rest.astype(np.float32).astype(ml_dtypes.bfloat16)


def sine_factors():
    sine = sine64()
    zero = np.zeros((BOX, BOX))
    high, low = high_low(np.block([[sine, zero], [zero, sine]]))
    y_right = np.concatenate(
        [np.concatenate([high, low], 1), np.concatenate([high, np.zeros_like(high)], 1)], 0
    )
    half = 2 * np.arange(TILES)
    rows = []
    for h in range(2):
        rows.append(np.concatenate([sine[np.ix_(half + h, half + h)], sine[np.ix_(half + h, half + 1 - h)]], 1))
    high, low = high_low(np.concatenate(rows, 0))
    return jnp.asarray(y_right), jnp.asarray(np.concatenate([high, high, low], 1))


def z_factors(grid_index):
    steps = jnp.arange(1, BOX + 1).astype(F32)
    eigen = 2.0 - 2.0 * jnp.cos(jnp.pi * steps / (BOX + 1))
    s = (eigen[:, None] + eigen[None, :] + MU2).reshape(TILES, LANES)[None]
    theta = jnp.log(1.0 + 0.5 * s + jnp.sqrt(s + 0.25 * s * s))

    def number(n):
        return jnp.asarray(n).reshape(-1).astype(F32)[:, None, None]

    def rest(n):
        return 1.0 - jnp.exp(-2.0 * theta * number(n))

    def fall(n):
        return jnp.exp(-theta * number(n))

    z = grid_index * PLANES + jnp.arange(PLANES)
    up = fall(1) * rest(z) / rest(z + 1)
    down = fall(1) * rest(63 - z) / rest(64 - z)
    scale = MU2 / (rest(1) * rest(65))
    middle = scale * fall(1) * rest(z + 1) * rest(64 - z)
    pair = grid_index // 2
    e = jnp.arange(1, PAIRS)
    other = (pair - e) % PAIRS
    below = e <= pair
    away = jnp.where(below, 8 * grid_index - 16 * other - 16, 16 * other - 8 * grid_index - 8)
    first = jnp.where(below, 16 * other + 16, 64 - 16 * other)
    last = jnp.where(below, 8 * grid_index, 56 - 8 * grid_index)
    carry = fall(away) * rest(first) / rest(last)
    edge = 16 * pair + 8
    past_up = fall(8) * rest(edge) / rest(edge + 8)
    past_down = fall(8) * rest(64 - edge) / rest(72 - edge)
    return jnp.concatenate([up, down, middle, carry, past_up, past_down], 0)


def lane_iota(rows):
    return lax.broadcasted_iota(jnp.int32, (rows, LANES), 1)


def split(value):
    high = value.astype(BF16)
    return high, (value - high.astype(F32)).astype(BF16)


def dot(left, right):
    return jnp.dot(left, right, preferred_element_type=F32)


def times_y(value, y_right):
    high, low = split(value)
    both = dot(jnp.concatenate([high, low], axis=1), y_right)
    return both[:, :LANES] + both[:, LANES:]


def times_x(planes, x_left, terms):
    value = jnp.concatenate(planes, axis=1)
    other = jnp.concatenate([pltpu.roll(p, BOX, 1) for p in planes], axis=1)
    data = jnp.concatenate([value, other], axis=0)
    if terms == 1:
        high = data.astype(BF16)
        both = dot(x_left[:, BOX:], jnp.concatenate([high, high], axis=0))
    else:
        high, low = split(data)
        both = dot(x_left, jnp.concatenate([high, low, high], axis=0))
    first = lane_iota(TILES) < BOX
    out = []
    for z in range(PLANES):
        tile = both[:, LANES * z : LANES * (z + 1)]
        out.append(jnp.where(first, tile[:TILES], tile[TILES:]))
    return out


def shifted(value, step_x, step_y, buffer):
    buffer[PAD * 8 : PAD * 8 + ROWS, :] = value
    flat = step_x * BOX + step_y
    tiles = flat >> 7
    lanes = flat & 127
    start = pl.multiple_of((tiles + PAD) * 8, 8)
    window = buffer[pl.ds(start, ROWS + 8), :]
    window = pltpu.roll(window, (LANES - lanes) & 127, 1)
    lane = lane_iota(ROWS)
    moved = jnp.where(lane < LANES - lanes, window[:ROWS], window[8:])
    y_new = (lane & (BOX - 1)) + step_y
    return jnp.where((y_new >= 0) & (y_new < BOX), moved, 0.0)


def clear_margins(buffer):
    zero = jnp.zeros((PAD * 8, LANES), F32)
    buffer[: PAD * 8, :] = zero
    buffer[PAD * 8 + ROWS :, :] = zero


def column_sums(value):
    return jnp.sum(value, axis=0, keepdims=True)


def forward(rho, tables, held, coeffs, ends, message, n):
    y_right, x_left, z_table = tables
    held[...] = times_y(rho, y_right[...])
    planes = times_x([held[pl.ds(z, TILES, stride=PLANES), :] for z in range(PLANES)], x_left[...], 1)
    for z in range(PLANES):
        coeffs[n, TILES * z : TILES * (z + 1), :] = planes[z]
    above = planes[0]
    for z in range(1, PLANES):
        above = z_table[UP + z] * above + planes[z]
    below = planes[PLANES - 1]
    for z in range(PLANES - 2, -1, -1):
        below = z_table[DOWN + z] * below + planes[z]
    both = jnp.concatenate([above, below], axis=0)
    ends[n] = both
    message[2 * TILES * n : 2 * TILES * (n + 1), :] = both.astype(BF16)


def halves(message, n):
    both = message[2 * TILES * n : 2 * TILES * (n + 1), :].astype(F32)
    return both[:TILES], both[TILES:]


def inverse(grid, near, sums, coeffs, tables, held, n):
    y_right, x_left, z_table = tables
    near_up, near_down = halves(near, n)
    upper = (grid & 1) == 1
    from_below = jnp.where(upper, near_up, 0.0)
    from_above = jnp.where(upper, 0.0, near_down)
    for e in range(1, PAIRS):
        below = e <= (grid >> 1)
        term = z_table[CARRY + e - 1] * sums[e - 1]
        from_below += jnp.where(below, term, 0.0)
        from_above += jnp.where(below, 0.0, term)
    planes = [coeffs[n, TILES * z : TILES * (z + 1), :] for z in range(PLANES)]
    ups = []
    for z in range(PLANES):
        from_below = z_table[UP + z] * from_below + planes[z]
        ups.append(from_below)
    solved = [None] * PLANES
    product = jnp.zeros((TILES, LANES), F32)
    for z in range(PLANES - 1, -1, -1):
        carried = z_table[DOWN + z] * from_above
        solved[z] = z_table[MIDDLE + z] * (ups[z] + carried)
        from_above = planes[z] + carried
        product += planes[z] * solved[z]
    full = times_y(jnp.concatenate(times_x(solved, x_left[...], 1), axis=0), y_right[...])
    for z in range(PLANES):
        held[pl.ds(z, TILES, stride=PLANES), :] = full[TILES * z : TILES * (z + 1)]
    return held[...], column_sums(product)


def pair_scalars(pairs, anchor, n):
    owner = jnp.maximum(pairs[0, n], 0)
    mate = jnp.maximum(pairs[1, n], 0)
    step_x = anchor[0, owner] - anchor[0, mate]
    step_y = anchor[1, owner] - anchor[1, mate]
    return pairs[1, n] >= 0, owner & (ORB_DEV - 1), step_x, step_y


def tile(box, t):
    return box[PLANES * t : PLANES * (t + 1)]


def rows_kernel(orb, orb_rows):
    for n in range(ORB_DEV):
        wide = orb[n].astype(F32)
        box = jnp.concatenate([wide[:, LANES * t : LANES * (t + 1)] for t in range(TILES)], axis=0)
        orb_rows[n] = box.astype(BF16)


def spread_kernel(pairs, orb, out):
    wide = [orb[n].astype(F32) for n in range(ORB_DEV)]
    place = lax.broadcasted_iota(jnp.int32, (EXTRA, LANES), 0) * 2 + lane_iota(EXTRA)
    partners = jnp.zeros((EXTRA, LANES), F32)
    for n in range(ENTRIES):
        here = (place == n) & (lane_iota(EXTRA) < 2)
        partners = jnp.where(here, pairs[1, n].astype(F32), partners)
    partners = partners.astype(BF16)
    for t in range(TILES):
        piece = jnp.concatenate([w[:, LANES * t : LANES * (t + 1)] for w in wide], axis=0)
        out[t, : ORB_DEV * PLANES, :] = piece.astype(BF16)
        out[t, ORB_DEV * PLANES :, :] = partners


def serve_kernel(partners, held, out, every):
    count = held.shape[0]
    for d in range(count):
        pieces = held[d, : ORB_DEV * PLANES, :].astype(F32)
        for n in range(ORB_DEV):
            every[ORB_DEV * d + n] = tile(pieces, n)

    def step(i, carry):
        for d in range(4):
            d += 4 * i
            pieces = [every[partners[ENTRIES * d + n]] for n in range(ENTRIES)]
            out[d] = jnp.concatenate(pieces, axis=0).astype(BF16)
        return carry

    lax.fori_loop(0, count // 4, step, 0)


def base_forward_kernel(orb_rows, y_right, x_left, z_table, coeffs, ends, message, *held):
    for n in range(ORB_DEV):
        box = orb_rows[n].astype(F32)
        forward(box * box, (y_right, x_left, z_table), held[n], coeffs, ends, message, n)


def pair_forward_kernel(start, pairs, anchor, orb_rows, fetched, y_right, x_left, z_table, moved_out, coeffs, ends, message, *refs):
    count = moved_out.shape[0]
    buffers, held = refs[:count], refs[count:]
    for n in range(count):
        clear_margins(buffers[n])
    for m in range(0, count, 2):
        row = PLANES * (start + m)
        both = [fetched[t, row : row + 2 * PLANES, :].astype(F32) for t in range(TILES)]
        for n in (m, m + 1):
            _, owner, step_x, step_y = pair_scalars(pairs, anchor, start + n)
            mate = jnp.concatenate([tile(b, n - m) for b in both], axis=0)
            moved = shifted(mate, step_x, step_y, buffers[n])
            moved_out[n] = moved.astype(BF16)
            rho = orb_rows[owner].astype(F32) * moved
            forward(rho, (y_right, x_left, z_table), held[n], coeffs, ends, message, n)


def pair_up_kernel(grid, ends, near, z_table, *outs):
    pair, upper = grid[0] >> 1, (grid[0] & 1) == 1
    for n in range(ends.shape[0]):
        near_up, near_down = halves(near, n)
        mine = ends[n]
        mine_up, mine_down = mine[:TILES], mine[TILES:]
        low_up = jnp.where(upper, near_up, mine_up)
        high_up = jnp.where(upper, mine_up, near_up)
        low_down = jnp.where(upper, near_down, mine_down)
        high_down = jnp.where(upper, mine_down, near_down)
        up = (z_table[PAST_UP] * low_up + high_up).astype(BF16)
        down = (low_down + z_table[PAST_DOWN] * high_down).astype(BF16)
        for e in range(1, PAIRS):
            outs[e - 1][n] = jnp.where(pair + e < PAIRS, up, down)


def in_order(refs, n):
    return [refs[ORDER.index(e)][n].astype(F32) for e in range(1, PAIRS)]


def base_inverse_kernel(grid, near, *refs):
    sums, refs = refs[: PAIRS - 1], refs[PAIRS - 1 :]
    coeffs, orb_rows, y_right, x_left, z_table, total, energy, *held = refs
    tables = (y_right, x_left, z_table)
    for n in range(ORB_DEV):
        potential, value = inverse(grid[0], near, in_order(sums, n), coeffs, tables, held[n], n)
        total[n] = orb_rows[n].astype(F32) * potential
        energy[n : n + 1, :] = value


def pair_inverse_kernel(start, grid, pairs, anchor, near, *refs):
    sums, refs = refs[: PAIRS - 1], refs[PAIRS - 1 :]
    coeffs, orb_rows, moved, y_right, x_left, z_table, total_in, out_in, total, out, energy, *refs = refs
    count = moved.shape[0]
    buffers, held = refs[:count], refs[count:]
    tables = (y_right, x_left, z_table)
    for n in range(count):
        clear_margins(buffers[n])
    total[...] = total_in[...]
    if start:
        out[:, : PLANES * start, :] = out_in[:, : PLANES * start, :]
    for m in range(0, count, 2):
        backs = []
        for n in (m, m + 1):
            _, owner, step_x, step_y = pair_scalars(pairs, anchor, start + n)
            potential, value = inverse(grid[0], near, in_order(sums, n), coeffs, tables, held[n], n)
            energy[n : n + 1, :] = value
            backs.append(shifted(orb_rows[owner].astype(F32) * potential, -step_x, -step_y, buffers[n]))
        row = PLANES * (start + m)
        for t in range(TILES):
            piece = jnp.concatenate([tile(back, t) for back in backs], axis=0)
            out[t, row : row + 2 * PLANES, :] = piece.astype(BF16)
    for n in range(count):
        live, owner, _, _ = pair_scalars(pairs, anchor, start + n)
        total[owner] += jnp.where(live, moved[n].astype(F32) * held[n][...], 0.0)


def gather_kernel(partners, pairs, arrived, energy, out, energy_here, every_energy, *every):
    count = arrived.shape[0]
    spare = ORB_DEV * count
    for part in every:
        part[...] = jnp.zeros_like(part)

    def step(i, carry):
        for d in (2 * i, 2 * i + 1):
            for m in range(0, ENTRIES, 2):
                both = arrived[d, PLANES * m : PLANES * (m + 2), :].astype(F32)
                for n in (m, m + 1):
                    every[n % len(every)][partners[ENTRIES * d + n]] += tile(both, n - m)
        return carry

    lax.fori_loop(0, count // 2, step, 0)
    every_energy[...] = jnp.zeros_like(every_energy)
    first = lane_iota(1) == 0
    for n in range(ORB_DEV):
        energy_here[n : n + 1, :] = jnp.where(first, energy[n], 0.0)
    for n in range(ENTRIES):
        mate = pairs[1, n]
        owner = pairs[0, n] & (ORB_DEV - 1)
        value = jnp.where(first & (mate >= 0), energy[ORB_DEV + n], 0.0)
        every_energy[pl.ds(jnp.where(mate >= 0, mate, spare), 1), :] += value
        energy_here[pl.ds(owner, 1), :] += value
    for d in range(count):
        pieces = [sum(part[ORB_DEV * d + n] for part in every) for n in range(ORB_DEV)]
        out[d, : ORB_DEV * PLANES, :] = jnp.concatenate(pieces, axis=0).astype(BF16)
        value = every_energy[ORB_DEV * d : ORB_DEV * (d + 1), :]
        high = value.astype(BF16).astype(F32)
        low = pltpu.roll(value - high, 1, 1)
        out[d, ORB_DEV * PLANES :, :] = jnp.where(lane_iota(ORB_DEV) == 1, low, high).astype(BF16)


def finish_kernel(arrived, total, energy, out, energy_out):
    sums = energy[...]
    for t in range(TILES):
        pieces = arrived[t, : ORB_DEV * PLANES, :].astype(F32)
        for n in range(ORB_DEV):
            here = total[n, PLANES * t : PLANES * (t + 1), :] + tile(pieces, n)
            out[n, :, LANES * t : LANES * (t + 1)] = here.astype(BF16)
        sums += arrived[t, ORB_DEV * PLANES :, :].astype(F32)
    for n in range(ORB_DEV):
        energy_out[n] = jnp.sum(sums[n : n + 1, :])


VMEM = pl.BlockSpec(memory_space=pltpu.VMEM)
SMEM = pl.BlockSpec(memory_space=pltpu.SMEM)
ANY = pl.BlockSpec(memory_space=pl.ANY)
HELD = pltpu.VMEM((ROWS, LANES), F32)
SHIFT_BUFFER = pltpu.VMEM(((2 * PAD + TILES) * 8, LANES), F32)


def shape(*dims, dtype=BF16):
    return jax.ShapeDtypeStruct(dims, dtype)


def solve_shapes(count):
    return [
        shape(count, ROWS, LANES, dtype=F32),
        shape(count, 2 * TILES, LANES, dtype=F32),
        shape(count * 2 * TILES, LANES),
    ]


def call(kernel, out_shape, in_specs, scratch, name, micros, out_specs=None, aliases=None, limit=VMEM_LIMIT):
    return pl.pallas_call(
        kernel,
        out_shape=out_shape,
        in_specs=in_specs,
        out_specs=out_specs if out_specs is not None else jax.tree.map(lambda _: VMEM, out_shape),
        scratch_shapes=scratch,
        input_output_aliases=aliases or {},
        name=name,
        cost_estimate=pl.CostEstimate(flops=0, bytes_accessed=int(micros * 3.0e6), transcendentals=0),
        compiler_params=pltpu.CompilerParams(vmem_limit_bytes=limit),
    )


def local(orbitals, pair_list, box_anchor):
    devices = lax.axis_size("orb")
    grid_index = lax.axis_index("grid")
    grid = grid_index.astype(jnp.int32).reshape(1)
    y_right, x_left = sine_factors()
    z_table = z_factors(grid_index)
    tables = (y_right, x_left, z_table)
    spread = ORB_DEV * PLANES + EXTRA
    totals = shape(ORB_DEV, ROWS, LANES, dtype=F32)

    def to_all(blocks):
        return lax.all_to_all(blocks, "orb", split_axis=0, concat_axis=0, tiled=True)

    def to_near(message):
        return lax.ppermute(message, "grid", [(i, i ^ 1) for i in range(GRID)])

    def from_pairs(ends, near):
        outs = [shape(ends.shape[0], TILES, LANES)] * (PAIRS - 1)
        sums = call(pair_up_kernel, outs, [SMEM] + [VMEM] * 3, [], "pair_up", 1)(grid, ends, near, z_table)
        hops = [[(i, (i + 2 * e) % GRID) for i in range(GRID)] for e in ORDER]
        return [lax.ppermute(sums[e - 1], "grid", hop) for e, hop in zip(ORDER, hops)]

    pieces = call(
        spread_kernel, shape(devices, spread, LANES), [SMEM, VMEM], [], "spread", 1, limit=62 * 1024 * 1024
    )(pair_list, orbitals)
    orbitals, _ = lax.optimization_barrier((orbitals, pieces))
    orb_rows = call(rows_kernel, shape(ORB_DEV, ROWS, LANES), [VMEM], [], "rows", 1)(orbitals)
    pieces = to_all(pieces)
    base_coeffs, base_ends, message = call(
        base_forward_kernel, solve_shapes(ORB_DEV), [VMEM] * 4, [HELD] * ORB_DEV, "base_forward", 2
    )(orb_rows, *tables)
    pieces, base_near = lax.optimization_barrier((pieces, to_near(message)))
    partners = pieces[:, ORB_DEV * PLANES :, :2].astype(jnp.int32).reshape(-1)
    served = call(
        serve_kernel,
        shape(devices, ENTRIES * PLANES, LANES),
        [SMEM, VMEM],
        [pltpu.VMEM((devices * ORB_DEV, PLANES, LANES), F32)],
        "serve",
        2,
    )(jnp.maximum(partners, 0), pieces)
    fetched = to_all(served)
    base_sums = from_pairs(base_ends, base_near)
    fetched, base_sums = lax.optimization_barrier((fetched, base_sums))
    total, base_energy = call(
        base_inverse_kernel,
        [totals, shape(ORB_DEV, LANES, dtype=F32)],
        [SMEM] + [VMEM] * (PAIRS + 5),
        [HELD] * ORB_DEV,
        "base_inverse",
        2,
    )(grid, base_near, *base_sums, base_coeffs, orb_rows, *tables)

    parts = []
    for start, count in PARTS:
        moved, coeffs, ends, message = call(
            functools.partial(pair_forward_kernel, start),
            [shape(count, ROWS, LANES)] + solve_shapes(count),
            [SMEM] * 2 + [VMEM] * 5,
            [SHIFT_BUFFER] * count + [HELD] * count,
            "pair_forward",
            2,
        )(pair_list, box_anchor, orb_rows, fetched, *tables)
        parts.append((start, moved, coeffs, ends, to_near(message)))
    start, moved, coeffs, ends, near = parts[0]
    total, near = lax.optimization_barrier((total, near))
    parts[0] = (start, moved, coeffs, ends, near)
    parts = [(*part, from_pairs(part[3], part[4])) for part in parts]
    back, energy = served, [base_energy]
    for start, moved, coeffs, ends, near, sums in parts:
        count = moved.shape[0]
        total, back, value = call(
            functools.partial(pair_inverse_kernel, start),
            [totals, shape(devices, (start + count) * PLANES, LANES), shape(count, LANES, dtype=F32)],
            [SMEM] * 3 + [VMEM] * (PAIRS + 7) + [VMEM if start else ANY],
            [SHIFT_BUFFER] * count + [HELD] * count,
            "pair_inverse",
            3,
            aliases={PAIRS + 9: 0},
        )(grid, pair_list, box_anchor, near, *sums, coeffs, orb_rows, moved, *tables, total, back)
        energy.append(value)

    arrived = to_all(back)
    energy = lax.psum(jnp.sum(jnp.concatenate(energy), axis=1), "grid")
    due, energy = call(
        gather_kernel,
        [shape(devices, spread, LANES), shape(ORB_DEV, LANES, dtype=F32)],
        [SMEM] * 2 + [VMEM, SMEM],
        [pltpu.VMEM((devices * ORB_DEV + 8, LANES), F32)]
        + [pltpu.VMEM((devices * ORB_DEV + 1, PLANES, LANES), F32)] * 4,
        "gather",
        4,
    )(jnp.where(partners >= 0, partners, devices * ORB_DEV), pair_list, arrived, energy)
    return call(
        finish_kernel,
        [shape(*orbitals.shape), shape(ORB_DEV, dtype=F32)],
        [VMEM] * 3,
        [],
        "finish",
        3,
        out_specs=[VMEM, SMEM],
    )(to_all(due), total, energy)


def solution(mesh):
    return jax.shard_map(
        local,
        mesh=mesh,
        in_specs=(P("orb", "grid", None), P(None, "orb"), P()),
        out_specs=(P("orb", "grid", None), P("orb")),
        check_vma=False,
    )
```

```python
import functools

import jax
import jax.numpy as jnp
import ml_dtypes
import numpy as np
from jax import lax
from jax.experimental import pallas as pl
from jax.experimental.pallas import tpu as pltpu
from jax.sharding import PartitionSpec as P

BOX = 64
LANES = 128
TILES = BOX * BOX // LANES
PLANES = 8
ROWS = TILES * PLANES
GRID = 8
PAIRS = GRID // 2
ORDER = (2, 1, 3)
UP, DOWN, MIDDLE, CARRY, PAST_UP, PAST_DOWN = 0, 8, 16, 24, 27, 28
ORB_DEV = 8
ENTRIES = 16
EXTRA = 8
PARTS = ((0, 8), (8, 8))
PAD = 10
MU2 = 0.02
BF16 = jnp.bfloat16
F32 = jnp.float32
VMEM_LIMIT = 40 * 1024 * 1024


def sine64():
    steps = np.arange(1, BOX + 1, dtype=np.float64)
    return np.sqrt(2.0 / (BOX + 1)) * np.sin(np.pi * steps[:, None] * steps[None, :] / (BOX + 1))


def high_low(table):
    high = table.astype(np.float32).astype(ml_dtypes.bfloat16)
    rest = table - high.astype(np.float64)
    return high, rest.astype(np.float32).astype(ml_dtypes.bfloat16)


def sine_factors():
    sine = sine64()
    zero = np.zeros((BOX, BOX))
    high, low = high_low(np.block([[sine, zero], [zero, sine]]))
    y_right = np.concatenate(
        [np.concatenate([high, low], 1), np.concatenate([high, np.zeros_like(high)], 1)], 0
    )
    half = 2 * np.arange(TILES)
    rows = []
    for h in range(2):
        rows.append(np.concatenate([sine[np.ix_(half + h, half + h)], sine[np.ix_(half + h, half + 1 - h)]], 1))
    high, low = high_low(np.concatenate(rows, 0))
    return jnp.asarray(y_right), jnp.asarray(np.concatenate([high, high, low], 1))


def z_factors(grid_index):
    steps = jnp.arange(1, BOX + 1).astype(F32)
    eigen = 2.0 - 2.0 * jnp.cos(jnp.pi * steps / (BOX + 1))
    s = (eigen[:, None] + eigen[None, :] + MU2).reshape(TILES, LANES)[None]
    theta = jnp.log(1.0 + 0.5 * s + jnp.sqrt(s + 0.25 * s * s))

    def number(n):
        return jnp.asarray(n).reshape(-1).astype(F32)[:, None, None]

    def rest(n):
        return 1.0 - jnp.exp(-2.0 * theta * number(n))

    def fall(n):
        return jnp.exp(-theta * number(n))

    z = grid_index * PLANES + jnp.arange(PLANES)
    up = fall(1) * rest(z) / rest(z + 1)
    down = fall(1) * rest(63 - z) / rest(64 - z)
    scale = MU2 / (rest(1) * rest(65))
    middle = scale * fall(1) * rest(z + 1) * rest(64 - z)
    pair = grid_index // 2
    e = jnp.arange(1, PAIRS)
    other = (pair - e) % PAIRS
    below = e <= pair
    away = jnp.where(below, 8 * grid_index - 16 * other - 16, 16 * other - 8 * grid_index - 8)
    first = jnp.where(below, 16 * other + 16, 64 - 16 * other)
    last = jnp.where(below, 8 * grid_index, 56 - 8 * grid_index)
    carry = fall(away) * rest(first) / rest(last)
    edge = 16 * pair + 8
    past_up = fall(8) * rest(edge) / rest(edge + 8)
    past_down = fall(8) * rest(64 - edge) / rest(72 - edge)
    return jnp.concatenate([up, down, middle, carry, past_up, past_down], 0)


def lane_iota(rows):
    return lax.broadcasted_iota(jnp.int32, (rows, LANES), 1)


def split(value):
    high = value.astype(BF16)
    return high, (value - high.astype(F32)).astype(BF16)


def dot(left, right):
    return jnp.dot(left, right, preferred_element_type=F32)


def times_y(value, y_right):
    high, low = split(value)
    both = dot(jnp.concatenate([high, low], axis=1), y_right)
    return both[:, :LANES] + both[:, LANES:]


def times_x(planes, x_left, terms):
    value = jnp.concatenate(planes, axis=1)
    other = jnp.concatenate([pltpu.roll(p, BOX, 1) for p in planes], axis=1)
    data = jnp.concatenate([value, other], axis=0)
    if terms == 1:
        high = data.astype(BF16)
        both = dot(x_left[:, BOX:], jnp.concatenate([high, high], axis=0))
    else:
        high, low = split(data)
        both = dot(x_left, jnp.concatenate([high, low, high], axis=0))
    first = lane_iota(TILES) < BOX
    out = []
    for z in range(PLANES):
        tile = both[:, LANES * z : LANES * (z + 1)]
        out.append(jnp.where(first, tile[:TILES], tile[TILES:]))
    return out


def shifted(value, step_x, step_y, buffer):
    buffer[PAD * 8 : PAD * 8 + ROWS, :] = value
    flat = step_x * BOX + step_y
    tiles = flat >> 7
    lanes = flat & 127
    start = pl.multiple_of((tiles + PAD) * 8, 8)
    window = buffer[pl.ds(start, ROWS + 8), :]
    window = pltpu.roll(window, (LANES - lanes) & 127, 1)
    lane = lane_iota(ROWS)
    moved = jnp.where(lane < LANES - lanes, window[:ROWS], window[8:])
    y_new = (lane & (BOX - 1)) + step_y
    return jnp.where((y_new >= 0) & (y_new < BOX), moved, 0.0)


def clear_margins(buffer):
    zero = jnp.zeros((PAD * 8, LANES), F32)
    buffer[: PAD * 8, :] = zero
    buffer[PAD * 8 + ROWS :, :] = zero


def column_sums(value):
    return jnp.sum(value, axis=0, keepdims=True)


def forward(rho, tables, held, coeffs, ends, message, n):
    y_right, x_left, z_table = tables
    held[...] = times_y(rho, y_right[...])
    planes = times_x([held[pl.ds(z, TILES, stride=PLANES), :] for z in range(PLANES)], x_left[...], 1)
    for z in range(PLANES):
        coeffs[n, TILES * z : TILES * (z + 1), :] = planes[z]
    above = planes[0]
    for z in range(1, PLANES):
        above = z_table[UP + z] * above + planes[z]
    below = planes[PLANES - 1]
    for z in range(PLANES - 2, -1, -1):
        below = z_table[DOWN + z] * below + planes[z]
    both = jnp.concatenate([above, below], axis=0)
    ends[n] = both
    message[2 * TILES * n : 2 * TILES * (n + 1), :] = both.astype(BF16)


def halves(message, n):
    both = message[2 * TILES * n : 2 * TILES * (n + 1), :].astype(F32)
    return both[:TILES], both[TILES:]


def inverse(grid, near, sums, coeffs, tables, held, n):
    y_right, x_left, z_table = tables
    near_up, near_down = halves(near, n)
    upper = (grid & 1) == 1
    from_below = jnp.where(upper, near_up, 0.0)
    from_above = jnp.where(upper, 0.0, near_down)
    for e in range(1, PAIRS):
        below = e <= (grid >> 1)
        term = z_table[CARRY + e - 1] * sums[e - 1]
        from_below += jnp.where(below, term, 0.0)
        from_above += jnp.where(below, 0.0, term)
    planes = [coeffs[n, TILES * z : TILES * (z + 1), :] for z in range(PLANES)]
    ups = []
    for z in range(PLANES):
        from_below = z_table[UP + z] * from_below + planes[z]
        ups.append(from_below)
    solved = [None] * PLANES
    product = jnp.zeros((TILES, LANES), F32)
    for z in range(PLANES - 1, -1, -1):
        carried = z_table[DOWN + z] * from_above
        solved[z] = z_table[MIDDLE + z] * (ups[z] + carried)
        from_above = planes[z] + carried
        product += planes[z] * solved[z]
    full = times_y(jnp.concatenate(times_x(solved, x_left[...], 1), axis=0), y_right[...])
    for z in range(PLANES):
        held[pl.ds(z, TILES, stride=PLANES), :] = full[TILES * z : TILES * (z + 1)]
    return held[...], column_sums(product)


def pair_scalars(pairs, anchor, n):
    owner = jnp.maximum(pairs[0, n], 0)
    mate = jnp.maximum(pairs[1, n], 0)
    step_x = anchor[0, owner] - anchor[0, mate]
    step_y = anchor[1, owner] - anchor[1, mate]
    return pairs[1, n] >= 0, owner & (ORB_DEV - 1), step_x, step_y


def tile(box, t):
    return box[PLANES * t : PLANES * (t + 1)]


def rows_kernel(orb, orb_rows):
    for n in range(ORB_DEV):
        wide = orb[n].astype(F32)
        box = jnp.concatenate([wide[:, LANES * t : LANES * (t + 1)] for t in range(TILES)], axis=0)
        orb_rows[n] = box.astype(BF16)


def spread_kernel(pairs, orb, out):
    wide = [orb[n].astype(F32) for n in range(ORB_DEV)]
    place = lax.broadcasted_iota(jnp.int32, (EXTRA, LANES), 0) * 2 + lane_iota(EXTRA)
    partners = jnp.zeros((EXTRA, LANES), F32)
    for n in range(ENTRIES):
        here = (place == n) & (lane_iota(EXTRA) < 2)
        partners = jnp.where(here, pairs[1, n].astype(F32), partners)
    partners = partners.astype(BF16)
    for t in range(TILES):
        piece = jnp.concatenate([w[:, LANES * t : LANES * (t + 1)] for w in wide], axis=0)
        out[t, : ORB_DEV * PLANES, :] = piece.astype(BF16)
        out[t, ORB_DEV * PLANES :, :] = partners


def serve_kernel(partners, held, out, every):
    count = held.shape[0]
    for d in range(count):
        pieces = held[d, : ORB_DEV * PLANES, :].astype(F32)
        for n in range(ORB_DEV):
            every[ORB_DEV * d + n] = tile(pieces, n)

    for d in range(count):
        pieces = [every[partners[ENTRIES * d + n]] for n in range(ENTRIES)]
        out[d] = jnp.concatenate(pieces, axis=0).astype(BF16)


def base_forward_kernel(orb_rows, y_right, x_left, z_table, coeffs, ends, message, *held):
    for n in range(ORB_DEV):
        box = orb_rows[n].astype(F32)
        forward(box * box, (y_right, x_left, z_table), held[n], coeffs, ends, message, n)


def pair_forward_kernel(start, pairs, anchor, orb_rows, fetched, y_right, x_left, z_table, moved_out, coeffs, ends, message, *refs):
    count = moved_out.shape[0]
    buffers, held = refs[:count], refs[count:]
    for n in range(count):
        clear_margins(buffers[n])
    for m in range(0, count, 2):
        row = PLANES * (start + m)
        both = [fetched[t, row : row + 2 * PLANES, :].astype(F32) for t in range(TILES)]
        for n in (m, m + 1):
            _, owner, step_x, step_y = pair_scalars(pairs, anchor, start + n)
            mate = jnp.concatenate([tile(b, n - m) for b in both], axis=0)
            moved = shifted(mate, step_x, step_y, buffers[n])
            moved_out[n] = moved.astype(BF16)
            rho = orb_rows[owner].astype(F32) * moved
            forward(rho, (y_right, x_left, z_table), held[n], coeffs, ends, message, n)


def pair_up_kernel(grid, ends, near, z_table, *outs):
    pair, upper = grid[0] >> 1, (grid[0] & 1) == 1
    for n in range(ends.shape[0]):
        near_up, near_down = halves(near, n)
        mine = ends[n]
        mine_up, mine_down = mine[:TILES], mine[TILES:]
        low_up = jnp.where(upper, near_up, mine_up)
        high_up = jnp.where(upper, mine_up, near_up)
        low_down = jnp.where(upper, near_down, mine_down)
        high_down = jnp.where(upper, mine_down, near_down)
        up = (z_table[PAST_UP] * low_up + high_up).astype(BF16)
        down = (low_down + z_table[PAST_DOWN] * high_down).astype(BF16)
        for e in range(1, PAIRS):
            outs[e - 1][n] = jnp.where(pair + e < PAIRS, up, down)


def in_order(refs, n):
    return [refs[ORDER.index(e)][n].astype(F32) for e in range(1, PAIRS)]


def base_inverse_kernel(grid, near, *refs):
    sums, refs = refs[: PAIRS - 1], refs[PAIRS - 1 :]
    coeffs, orb_rows, y_right, x_left, z_table, total, energy, *held = refs
    tables = (y_right, x_left, z_table)
    for n in range(ORB_DEV):
        potential, value = inverse(grid[0], near, in_order(sums, n), coeffs, tables, held[n], n)
        total[n] = orb_rows[n].astype(F32) * potential
        energy[n : n + 1, :] = value


def pair_inverse_kernel(start, grid, pairs, anchor, near, *refs):
    sums, refs = refs[: PAIRS - 1], refs[PAIRS - 1 :]
    coeffs, orb_rows, moved, y_right, x_left, z_table, total_in, out_in, total, out, energy, *refs = refs
    count = moved.shape[0]
    buffers, held = refs[:count], refs[count:]
    tables = (y_right, x_left, z_table)
    for n in range(count):
        clear_margins(buffers[n])
    total[...] = total_in[...]
    if start:
        out[:, : PLANES * start, :] = out_in[:, : PLANES * start, :]
    for m in range(0, count, 2):
        backs = []
        for n in (m, m + 1):
            _, owner, step_x, step_y = pair_scalars(pairs, anchor, start + n)
            potential, value = inverse(grid[0], near, in_order(sums, n), coeffs, tables, held[n], n)
            energy[n : n + 1, :] = value
            backs.append(shifted(orb_rows[owner].astype(F32) * potential, -step_x, -step_y, buffers[n]))
        row = PLANES * (start + m)
        for t in range(TILES):
            piece = jnp.concatenate([tile(back, t) for back in backs], axis=0)
            out[t, row : row + 2 * PLANES, :] = piece.astype(BF16)
    for n in range(count):
        live, owner, _, _ = pair_scalars(pairs, anchor, start + n)
        total[owner] += jnp.where(live, moved[n].astype(F32) * held[n][...], 0.0)


def gather_kernel(partners, pairs, arrived, energy, out, energy_here, every_energy, *every):
    count = arrived.shape[0]
    spare = ORB_DEV * count
    for part in every:
        part[...] = jnp.zeros_like(part)

    def step(i, carry):
        for d in [8 * i + j for j in range(8)]:
            for m in range(0, ENTRIES, 2):
                both = arrived[d, PLANES * m : PLANES * (m + 2), :].astype(F32)
                for n in (m, m + 1):
                    every[n % len(every)][partners[ENTRIES * d + n]] += tile(both, n - m)
        return carry

    lax.fori_loop(0, count // 8, step, 0)
    every_energy[...] = jnp.zeros_like(every_energy)
    first = lane_iota(1) == 0
    for n in range(ORB_DEV):
        energy_here[n : n + 1, :] = jnp.where(first, energy[n], 0.0)
    for n in range(ENTRIES):
        mate = pairs[1, n]
        owner = pairs[0, n] & (ORB_DEV - 1)
        value = jnp.where(first & (mate >= 0), energy[ORB_DEV + n], 0.0)
        every_energy[pl.ds(jnp.where(mate >= 0, mate, spare), 1), :] += value
        energy_here[pl.ds(owner, 1), :] += value
    for d in range(count):
        pieces = [sum(part[ORB_DEV * d + n] for part in every) for n in range(ORB_DEV)]
        out[d, : ORB_DEV * PLANES, :] = jnp.concatenate(pieces, axis=0).astype(BF16)
        value = every_energy[ORB_DEV * d : ORB_DEV * (d + 1), :]
        high = value.astype(BF16).astype(F32)
        low = pltpu.roll(value - high, 1, 1)
        out[d, ORB_DEV * PLANES :, :] = jnp.where(lane_iota(ORB_DEV) == 1, low, high).astype(BF16)


def finish_kernel(arrived, total, energy, out, energy_out):
    sums = energy[...]
    for t in range(TILES):
        pieces = arrived[t, : ORB_DEV * PLANES, :].astype(F32)
        for n in range(ORB_DEV):
            here = total[n, PLANES * t : PLANES * (t + 1), :] + tile(pieces, n)
            out[n, :, LANES * t : LANES * (t + 1)] = here.astype(BF16)
        sums += arrived[t, ORB_DEV * PLANES :, :].astype(F32)
    for n in range(ORB_DEV):
        energy_out[n] = jnp.sum(sums[n : n + 1, :])


VMEM = pl.BlockSpec(memory_space=pltpu.VMEM)
SMEM = pl.BlockSpec(memory_space=pltpu.SMEM)
ANY = pl.BlockSpec(memory_space=pl.ANY)
HELD = pltpu.VMEM((ROWS, LANES), F32)
SHIFT_BUFFER = pltpu.VMEM(((2 * PAD + TILES) * 8, LANES), F32)


def shape(*dims, dtype=BF16):
    return jax.ShapeDtypeStruct(dims, dtype)


def solve_shapes(count):
    return [
        shape(count, ROWS, LANES, dtype=F32),
        shape(count, 2 * TILES, LANES, dtype=F32),
        shape(count * 2 * TILES, LANES),
    ]


def call(kernel, out_shape, in_specs, scratch, name, micros, out_specs=None, aliases=None, limit=VMEM_LIMIT):
    return pl.pallas_call(
        kernel,
        out_shape=out_shape,
        in_specs=in_specs,
        out_specs=out_specs if out_specs is not None else jax.tree.map(lambda _: VMEM, out_shape),
        scratch_shapes=scratch,
        input_output_aliases=aliases or {},
        name=name,
        cost_estimate=pl.CostEstimate(flops=0, bytes_accessed=int(micros * 3.0e6), transcendentals=0),
        compiler_params=pltpu.CompilerParams(vmem_limit_bytes=limit),
    )


def local(orbitals, pair_list, box_anchor):
    devices = lax.axis_size("orb")
    grid_index = lax.axis_index("grid")
    grid = grid_index.astype(jnp.int32).reshape(1)
    y_right, x_left = sine_factors()
    z_table = z_factors(grid_index)
    tables = (y_right, x_left, z_table)
    spread = ORB_DEV * PLANES + EXTRA
    totals = shape(ORB_DEV, ROWS, LANES, dtype=F32)

    def to_all(blocks):
        return lax.all_to_all(blocks, "orb", split_axis=0, concat_axis=0, tiled=True)

    def to_near(message):
        return lax.ppermute(message, "grid", [(i, i ^ 1) for i in range(GRID)])

    def from_pairs(ends, near):
        outs = [shape(ends.shape[0], TILES, LANES)] * (PAIRS - 1)
        sums = call(pair_up_kernel, outs, [SMEM] + [VMEM] * 3, [], "pair_up", 1)(grid, ends, near, z_table)
        hops = [[(i, (i + 2 * e) % GRID) for i in range(GRID)] for e in ORDER]
        return [lax.ppermute(sums[e - 1], "grid", hop) for e, hop in zip(ORDER, hops)]

    pieces = call(
        spread_kernel, shape(devices, spread, LANES), [SMEM, VMEM], [], "spread", 1, limit=62 * 1024 * 1024
    )(pair_list, orbitals)
    orbitals, _ = lax.optimization_barrier((orbitals, pieces))
    orb_rows = call(rows_kernel, shape(ORB_DEV, ROWS, LANES), [VMEM], [], "rows", 1)(orbitals)
    pieces = to_all(pieces)
    base_coeffs, base_ends, message = call(
        base_forward_kernel, solve_shapes(ORB_DEV), [VMEM] * 4, [HELD] * ORB_DEV, "base_forward", 2
    )(orb_rows, *tables)
    pieces, base_near = lax.optimization_barrier((pieces, to_near(message)))
    partners = pieces[:, ORB_DEV * PLANES :, :2].astype(jnp.int32).reshape(-1)
    served = call(
        serve_kernel,
        shape(devices, ENTRIES * PLANES, LANES),
        [SMEM, VMEM],
        [pltpu.VMEM((devices * ORB_DEV, PLANES, LANES), F32)],
        "serve",
        2,
    )(jnp.maximum(partners, 0), pieces)
    fetched = to_all(served)
    base_sums = from_pairs(base_ends, base_near)
    fetched, base_sums = lax.optimization_barrier((fetched, base_sums))
    total, base_energy = call(
        base_inverse_kernel,
        [totals, shape(ORB_DEV, LANES, dtype=F32)],
        [SMEM] + [VMEM] * (PAIRS + 5),
        [HELD] * ORB_DEV,
        "base_inverse",
        2,
    )(grid, base_near, *base_sums, base_coeffs, orb_rows, *tables)

    parts = []
    for start, count in PARTS:
        moved, coeffs, ends, message = call(
            functools.partial(pair_forward_kernel, start),
            [shape(count, ROWS, LANES)] + solve_shapes(count),
            [SMEM] * 2 + [VMEM] * 5,
            [SHIFT_BUFFER] * count + [HELD] * count,
            "pair_forward",
            2,
        )(pair_list, box_anchor, orb_rows, fetched, *tables)
        parts.append((start, moved, coeffs, ends, to_near(message)))
    start, moved, coeffs, ends, near = parts[0]
    total, near = lax.optimization_barrier((total, near))
    parts[0] = (start, moved, coeffs, ends, near)
    parts = [(*part, from_pairs(part[3], part[4])) for part in parts]
    back, energy = served, [base_energy]
    for start, moved, coeffs, ends, near, sums in parts:
        count = moved.shape[0]
        total, back, value = call(
            functools.partial(pair_inverse_kernel, start),
            [totals, shape(devices, (start + count) * PLANES, LANES), shape(count, LANES, dtype=F32)],
            [SMEM] * 3 + [VMEM] * (PAIRS + 7) + [VMEM if start else ANY],
            [SHIFT_BUFFER] * count + [HELD] * count,
            "pair_inverse",
            3,
            aliases={PAIRS + 9: 0},
        )(grid, pair_list, box_anchor, near, *sums, coeffs, orb_rows, moved, *tables, total, back)
        energy.append(value)

    arrived = to_all(back)
    energy = lax.psum(jnp.sum(jnp.concatenate(energy), axis=1), "grid")
    due, energy = call(
        gather_kernel,
        [shape(devices, spread, LANES), shape(ORB_DEV, LANES, dtype=F32)],
        [SMEM] * 2 + [VMEM, SMEM],
        [pltpu.VMEM((devices * ORB_DEV + 8, LANES), F32)]
        + [pltpu.VMEM((devices * ORB_DEV + 1, PLANES, LANES), F32)] * 4,
        "gather",
        4,
    )(jnp.where(partners >= 0, partners, devices * ORB_DEV), pair_list, arrived, energy)
    return call(
        finish_kernel,
        [shape(*orbitals.shape), shape(ORB_DEV, dtype=F32)],
        [VMEM] * 3,
        [],
        "finish",
        3,
        out_specs=[VMEM, SMEM],
    )(to_all(due), total, energy)


def solution(mesh):
    return jax.shard_map(
        local,
        mesh=mesh,
        in_specs=(P("orb", "grid", None), P(None, "orb"), P()),
        out_specs=(P("orb", "grid", None), P("orb")),
        check_vma=False,
    )
```

```python
import functools

import jax
import jax.numpy as jnp
import ml_dtypes
import numpy as np
from jax import lax
from jax.experimental import pallas as pl
from jax.experimental.pallas import tpu as pltpu
from jax.sharding import PartitionSpec as P

BOX = 64
LANES = 128
TILES = BOX * BOX // LANES
PLANES = 8
ROWS = TILES * PLANES
GRID = 8
PAIRS = GRID // 2
ORDER = (2, 1, 3)
UP, DOWN, MIDDLE, CARRY, PAST_UP, PAST_DOWN = 0, 8, 16, 24, 27, 28
ORB_DEV = 8
ENTRIES = 16
EXTRA = 8
PARTS = ((0, 8), (8, 8))
PAD = 10
MU2 = 0.02
BF16 = jnp.bfloat16
F32 = jnp.float32
VMEM_LIMIT = 40 * 1024 * 1024


def sine64():
    steps = np.arange(1, BOX + 1, dtype=np.float64)
    return np.sqrt(2.0 / (BOX + 1)) * np.sin(np.pi * steps[:, None] * steps[None, :] / (BOX + 1))


def high_low(table):
    high = table.astype(np.float32).astype(ml_dtypes.bfloat16)
    rest = table - high.astype(np.float64)
    return high, rest.astype(np.float32).astype(ml_dtypes.bfloat16)


def sine_factors():
    sine = sine64()
    zero = np.zeros((BOX, BOX))
    high, low = high_low(np.block([[sine, zero], [zero, sine]]))
    y_right = np.concatenate(
        [np.concatenate([high, low], 1), np.concatenate([high, np.zeros_like(high)], 1)], 0
    )
    half = 2 * np.arange(TILES)
    rows = []
    for h in range(2):
        rows.append(np.concatenate([sine[np.ix_(half + h, half + h)], sine[np.ix_(half + h, half + 1 - h)]], 1))
    high, low = high_low(np.concatenate(rows, 0))
    return jnp.asarray(y_right), jnp.asarray(np.concatenate([high, high, low], 1))


def z_factors(grid_index):
    steps = jnp.arange(1, BOX + 1).astype(F32)
    eigen = 2.0 - 2.0 * jnp.cos(jnp.pi * steps / (BOX + 1))
    s = (eigen[:, None] + eigen[None, :] + MU2).reshape(TILES, LANES)[None]
    theta = jnp.log(1.0 + 0.5 * s + jnp.sqrt(s + 0.25 * s * s))

    def number(n):
        return jnp.asarray(n).reshape(-1).astype(F32)[:, None, None]

    def rest(n):
        return 1.0 - jnp.exp(-2.0 * theta * number(n))

    def fall(n):
        return jnp.exp(-theta * number(n))

    z = grid_index * PLANES + jnp.arange(PLANES)
    up = fall(1) * rest(z) / rest(z + 1)
    down = fall(1) * rest(63 - z) / rest(64 - z)
    scale = MU2 / (rest(1) * rest(65))
    middle = scale * fall(1) * rest(z + 1) * rest(64 - z)
    pair = grid_index // 2
    e = jnp.arange(1, PAIRS)
    other = (pair - e) % PAIRS
    below = e <= pair
    away = jnp.where(below, 8 * grid_index - 16 * other - 16, 16 * other - 8 * grid_index - 8)
    first = jnp.where(below, 16 * other + 16, 64 - 16 * other)
    last = jnp.where(below, 8 * grid_index, 56 - 8 * grid_index)
    carry = fall(away) * rest(first) / rest(last)
    edge = 16 * pair + 8
    past_up = fall(8) * rest(edge) / rest(edge + 8)
    past_down = fall(8) * rest(64 - edge) / rest(72 - edge)
    return jnp.concatenate([up, down, middle, carry, past_up, past_down], 0)


def lane_iota(rows):
    return lax.broadcasted_iota(jnp.int32, (rows, LANES), 1)


def split(value):
    high = value.astype(BF16)
    return high, (value - high.astype(F32)).astype(BF16)


def dot(left, right):
    return jnp.dot(left, right, preferred_element_type=F32)


def times_y(value, y_right):
    high, low = split(value)
    both = dot(jnp.concatenate([high, low], axis=1), y_right)
    return both[:, :LANES] + both[:, LANES:]


def times_x(planes, x_left, terms):
    value = jnp.concatenate(planes, axis=1)
    other = jnp.concatenate([pltpu.roll(p, BOX, 1) for p in planes], axis=1)
    data = jnp.concatenate([value, other], axis=0)
    if terms == 1:
        high = data.astype(BF16)
        both = dot(x_left[:, BOX:], jnp.concatenate([high, high], axis=0))
    else:
        high, low = split(data)
        both = dot(x_left, jnp.concatenate([high, low, high], axis=0))
    first = lane_iota(TILES) < BOX
    out = []
    for z in range(PLANES):
        tile = both[:, LANES * z : LANES * (z + 1)]
        out.append(jnp.where(first, tile[:TILES], tile[TILES:]))
    return out


def shifted(value, step_x, step_y, buffer):
    buffer[PAD * 8 : PAD * 8 + ROWS, :] = value
    flat = step_x * BOX + step_y
    tiles = flat >> 7
    lanes = flat & 127
    start = pl.multiple_of((tiles + PAD) * 8, 8)
    window = buffer[pl.ds(start, ROWS + 8), :]
    window = pltpu.roll(window, (LANES - lanes) & 127, 1)
    lane = lane_iota(ROWS)
    moved = jnp.where(lane < LANES - lanes, window[:ROWS], window[8:])
    y_new = (lane & (BOX - 1)) + step_y
    return jnp.where((y_new >= 0) & (y_new < BOX), moved, 0.0)


def clear_margins(buffer):
    zero = jnp.zeros((PAD * 8, LANES), F32)
    buffer[: PAD * 8, :] = zero
    buffer[PAD * 8 + ROWS :, :] = zero


def column_sums(value):
    return jnp.sum(value, axis=0, keepdims=True)


def forward(rho, tables, held, coeffs, ends, message, n):
    y_right, x_left, z_table = tables
    held[...] = times_y(rho, y_right[...])
    planes = times_x([held[pl.ds(z, TILES, stride=PLANES), :] for z in range(PLANES)], x_left[...], 1)
    for z in range(PLANES):
        coeffs[n, TILES * z : TILES * (z + 1), :] = planes[z]
    above = planes[0]
    for z in range(1, PLANES):
        above = z_table[UP + z] * above + planes[z]
    below = planes[PLANES - 1]
    for z in range(PLANES - 2, -1, -1):
        below = z_table[DOWN + z] * below + planes[z]
    both = jnp.concatenate([above, below], axis=0)
    ends[n] = both
    message[2 * TILES * n : 2 * TILES * (n + 1), :] = both.astype(BF16)


def halves(message, n):
    both = message[2 * TILES * n : 2 * TILES * (n + 1), :].astype(F32)
    return both[:TILES], both[TILES:]


def inverse(grid, near, sums, coeffs, tables, held, n):
    y_right, x_left, z_table = tables
    near_up, near_down = halves(near, n)
    upper = (grid & 1) == 1
    from_below = jnp.where(upper, near_up, 0.0)
    from_above = jnp.where(upper, 0.0, near_down)
    for e in range(1, PAIRS):
        below = e <= (grid >> 1)
        term = z_table[CARRY + e - 1] * sums[e - 1]
        from_below += jnp.where(below, term, 0.0)
        from_above += jnp.where(below, 0.0, term)
    planes = [coeffs[n, TILES * z : TILES * (z + 1), :] for z in range(PLANES)]
    ups = []
    for z in range(PLANES):
        from_below = z_table[UP + z] * from_below + planes[z]
        ups.append(from_below)
    solved = [None] * PLANES
    product = jnp.zeros((TILES, LANES), F32)
    for z in range(PLANES - 1, -1, -1):
        carried = z_table[DOWN + z] * from_above
        solved[z] = z_table[MIDDLE + z] * (ups[z] + carried)
        from_above = planes[z] + carried
        product += planes[z] * solved[z]
    full = times_y(jnp.concatenate(times_x(solved, x_left[...], 1), axis=0), y_right[...])
    for z in range(PLANES):
        held[pl.ds(z, TILES, stride=PLANES), :] = full[TILES * z : TILES * (z + 1)]
    return held[...], column_sums(product)


def pair_scalars(pairs, anchor, n):
    owner = jnp.maximum(pairs[0, n], 0)
    mate = jnp.maximum(pairs[1, n], 0)
    step_x = anchor[0, owner] - anchor[0, mate]
    step_y = anchor[1, owner] - anchor[1, mate]
    return pairs[1, n] >= 0, owner & (ORB_DEV - 1), step_x, step_y


def tile(box, t):
    return box[PLANES * t : PLANES * (t + 1)]


def rows_kernel(orb, orb_rows):
    for n in range(ORB_DEV):
        wide = orb[n].astype(F32)
        box = jnp.concatenate([wide[:, LANES * t : LANES * (t + 1)] for t in range(TILES)], axis=0)
        orb_rows[n] = box.astype(BF16)


def spread_kernel(pairs, orb, out):
    wide = [orb[n].astype(F32) for n in range(ORB_DEV)]
    place = lax.broadcasted_iota(jnp.int32, (EXTRA, LANES), 0) * 2 + lane_iota(EXTRA)
    partners = jnp.zeros((EXTRA, LANES), F32)
    for n in range(ENTRIES):
        here = (place == n) & (lane_iota(EXTRA) < 2)
        partners = jnp.where(here, pairs[1, n].astype(F32), partners)
    partners = partners.astype(BF16)
    for t in range(TILES):
        piece = jnp.concatenate([w[:, LANES * t : LANES * (t + 1)] for w in wide], axis=0)
        out[t, : ORB_DEV * PLANES, :] = piece.astype(BF16)
        out[t, ORB_DEV * PLANES :, :] = partners


def serve_kernel(partners, held, out, every):
    count = held.shape[0]
    for d in range(count):
        pieces = held[d, : ORB_DEV * PLANES, :].astype(F32)
        for n in range(ORB_DEV):
            every[ORB_DEV * d + n] = tile(pieces, n)

    def step(i, carry):
        for d in range(4):
            d += 4 * i
            pieces = [every[partners[ENTRIES * d + n]] for n in range(ENTRIES)]
            out[d] = jnp.concatenate(pieces, axis=0).astype(BF16)
        return carry

    lax.fori_loop(0, count // 4, step, 0)


def base_forward_kernel(orb_rows, y_right, x_left, z_table, coeffs, ends, message, *held):
    for n in range(ORB_DEV):
        box = orb_rows[n].astype(F32)
        forward(box * box, (y_right, x_left, z_table), held[n], coeffs, ends, message, n)


def pair_forward_kernel(start, pairs, anchor, orb_rows, fetched, y_right, x_left, z_table, moved_out, coeffs, ends, message, *refs):
    count = moved_out.shape[0]
    buffers, held = refs[:count], refs[count:]
    for n in range(count):
        clear_margins(buffers[n])
    for m in range(0, count, 2):
        row = PLANES * (start + m)
        both = [fetched[t, row : row + 2 * PLANES, :].astype(F32) for t in range(TILES)]
        for n in (m, m + 1):
            _, owner, step_x, step_y = pair_scalars(pairs, anchor, start + n)
            mate = jnp.concatenate([tile(b, n - m) for b in both], axis=0)
            moved = shifted(mate, step_x, step_y, buffers[n])
            moved_out[n] = moved.astype(BF16)
            rho = orb_rows[owner].astype(F32) * moved
            forward(rho, (y_right, x_left, z_table), held[n], coeffs, ends, message, n)


def pair_up_kernel(grid, ends, near, z_table, *outs):
    pair, upper = grid[0] >> 1, (grid[0] & 1) == 1
    for n in range(ends.shape[0]):
        near_up, near_down = halves(near, n)
        mine = ends[n]
        mine_up, mine_down = mine[:TILES], mine[TILES:]
        low_up = jnp.where(upper, near_up, mine_up)
        high_up = jnp.where(upper, mine_up, near_up)
        low_down = jnp.where(upper, near_down, mine_down)
        high_down = jnp.where(upper, mine_down, near_down)
        up = (z_table[PAST_UP] * low_up + high_up).astype(BF16)
        down = (low_down + z_table[PAST_DOWN] * high_down).astype(BF16)
        for e in range(1, PAIRS):
            outs[e - 1][n] = jnp.where(pair + e < PAIRS, up, down)


def in_order(refs, n):
    return [refs[ORDER.index(e)][n].astype(F32) for e in range(1, PAIRS)]


def base_inverse_kernel(grid, near, *refs):
    sums, refs = refs[: PAIRS - 1], refs[PAIRS - 1 :]
    coeffs, orb_rows, y_right, x_left, z_table, total, energy, *held = refs
    tables = (y_right, x_left, z_table)
    for n in range(ORB_DEV):
        potential, value = inverse(grid[0], near, in_order(sums, n), coeffs, tables, held[n], n)
        total[n] = orb_rows[n].astype(F32) * potential
        energy[n : n + 1, :] = value


def pair_inverse_kernel(start, grid, pairs, anchor, near, *refs):
    sums, refs = refs[: PAIRS - 1], refs[PAIRS - 1 :]
    coeffs, orb_rows, moved, y_right, x_left, z_table, total_in, out_in, total, out, energy, *refs = refs
    count = moved.shape[0]
    buffers, held = refs[:count], refs[count:]
    tables = (y_right, x_left, z_table)
    for n in range(count):
        clear_margins(buffers[n])
    total[...] = total_in[...]
    if start:
        out[:, : PLANES * start, :] = out_in[:, : PLANES * start, :]
    for m in range(0, count, 2):
        backs = []
        for n in (m, m + 1):
            _, owner, step_x, step_y = pair_scalars(pairs, anchor, start + n)
            potential, value = inverse(grid[0], near, in_order(sums, n), coeffs, tables, held[n], n)
            energy[n : n + 1, :] = value
            backs.append(shifted(orb_rows[owner].astype(F32) * potential, -step_x, -step_y, buffers[n]))
        row = PLANES * (start + m)
        for t in range(TILES):
            piece = jnp.concatenate([tile(back, t) for back in backs], axis=0)
            out[t, row : row + 2 * PLANES, :] = piece.astype(BF16)
    for n in range(count):
        live, owner, _, _ = pair_scalars(pairs, anchor, start + n)
        total[owner] += jnp.where(live, moved[n].astype(F32) * held[n][...], 0.0)


def gather_kernel(partners, pairs, arrived, energy, out, energy_here, every_energy, *every):
    count = arrived.shape[0]
    spare = ORB_DEV * count
    for part in every:
        part[...] = jnp.zeros_like(part)

    def step(i, carry):
        for d in (2 * i, 2 * i + 1):
            for m in range(0, ENTRIES, 2):
                both = arrived[d, PLANES * m : PLANES * (m + 2), :].astype(F32)
                for n in (m, m + 1):
                    every[n % len(every)][partners[ENTRIES * d + n]] += tile(both, n - m)
        return carry

    lax.fori_loop(0, count // 2, step, 0)
    every_energy[...] = jnp.zeros_like(every_energy)
    first = lane_iota(1) == 0
    for n in range(ORB_DEV):
        energy_here[n : n + 1, :] = jnp.where(first, energy[n], 0.0)
    for n in range(ENTRIES):
        mate = pairs[1, n]
        owner = pairs[0, n] & (ORB_DEV - 1)
        value = jnp.where(first & (mate >= 0), energy[ORB_DEV + n], 0.0)
        every_energy[pl.ds(jnp.where(mate >= 0, mate, spare), 1), :] += value
        energy_here[pl.ds(owner, 1), :] += value
    for d in range(count):
        pieces = [sum(part[ORB_DEV * d + n] for part in every) for n in range(ORB_DEV)]
        out[d, : ORB_DEV * PLANES, :] = jnp.concatenate(pieces, axis=0).astype(BF16)
        value = every_energy[ORB_DEV * d : ORB_DEV * (d + 1), :]
        high = value.astype(BF16).astype(F32)
        low = pltpu.roll(value - high, 1, 1)
        out[d, ORB_DEV * PLANES :, :] = jnp.where(lane_iota(ORB_DEV) == 1, low, high).astype(BF16)


def finish_kernel(arrived, total, energy, out, energy_out):
    sums = energy[...]
    for t in range(TILES):
        pieces = arrived[t, : ORB_DEV * PLANES, :].astype(F32)
        for n in range(ORB_DEV):
            here = total[n, PLANES * t : PLANES * (t + 1), :] + tile(pieces, n)
            out[n, :, LANES * t : LANES * (t + 1)] = here.astype(BF16)
        sums += arrived[t, ORB_DEV * PLANES :, :].astype(F32)
    for n in range(ORB_DEV):
        energy_out[n] = jnp.sum(sums[n : n + 1, :])


VMEM = pl.BlockSpec(memory_space=pltpu.VMEM)
SMEM = pl.BlockSpec(memory_space=pltpu.SMEM)
ANY = pl.BlockSpec(memory_space=pl.ANY)
HELD = pltpu.VMEM((ROWS, LANES), F32)
SHIFT_BUFFER = pltpu.VMEM(((2 * PAD + TILES) * 8, LANES), F32)


def shape(*dims, dtype=BF16):
    return jax.ShapeDtypeStruct(dims, dtype)


def solve_shapes(count):
    return [
        shape(count, ROWS, LANES, dtype=F32),
        shape(count, 2 * TILES, LANES, dtype=F32),
        shape(count * 2 * TILES, LANES),
    ]


def call(kernel, out_shape, in_specs, scratch, name, micros, out_specs=None, aliases=None, limit=VMEM_LIMIT):
    return pl.pallas_call(
        kernel,
        out_shape=out_shape,
        in_specs=in_specs,
        out_specs=out_specs if out_specs is not None else jax.tree.map(lambda _: VMEM, out_shape),
        scratch_shapes=scratch,
        input_output_aliases=aliases or {},
        name=name,
        cost_estimate=pl.CostEstimate(flops=0, bytes_accessed=int(micros * 3.0e6), transcendentals=0),
        compiler_params=pltpu.CompilerParams(vmem_limit_bytes=limit),
    )


def local(orbitals, pair_list, box_anchor):
    devices = lax.axis_size("orb")
    grid_index = lax.axis_index("grid")
    grid = grid_index.astype(jnp.int32).reshape(1)
    y_right, x_left = sine_factors()
    z_table = z_factors(grid_index)
    tables = (y_right, x_left, z_table)
    spread = ORB_DEV * PLANES + EXTRA
    totals = shape(ORB_DEV, ROWS, LANES, dtype=F32)

    def to_all(blocks):
        return lax.all_to_all(blocks, "orb", split_axis=0, concat_axis=0, tiled=True)

    def to_near(message):
        return lax.ppermute(message, "grid", [(i, i ^ 1) for i in range(GRID)])

    def from_pairs(ends, near, back=False):
        outs = [shape(ends.shape[0], TILES, LANES)] * (PAIRS - 1)
        sums = call(pair_up_kernel, outs, [SMEM] + [VMEM] * 3, [], "pair_up", 1)(grid, ends, near, z_table)
        if back:
            hop = [(i, (i + 6) % GRID) for i in range(GRID)]
            got = lax.ppermute(jnp.concatenate([sums[2], sums[1]]), "grid", hop)
            count = ends.shape[0]
            ahead = lax.ppermute(sums[0], "grid", [(i, (i + 2) % GRID) for i in range(GRID)])
            return [lax.ppermute(got[count:], "grid", hop), ahead, got[:count]]
        hops = [[(i, (i + 2 * e) % GRID) for i in range(GRID)] for e in ORDER]
        return [lax.ppermute(sums[e - 1], "grid", hop) for e, hop in zip(ORDER, hops)]

    pieces = call(
        spread_kernel, shape(devices, spread, LANES), [SMEM, VMEM], [], "spread", 1, limit=62 * 1024 * 1024
    )(pair_list, orbitals)
    orbitals, _ = lax.optimization_barrier((orbitals, pieces))
    orb_rows = call(rows_kernel, shape(ORB_DEV, ROWS, LANES), [VMEM], [], "rows", 1)(orbitals)
    pieces = to_all(pieces)
    base_coeffs, base_ends, message = call(
        base_forward_kernel, solve_shapes(ORB_DEV), [VMEM] * 4, [HELD] * ORB_DEV, "base_forward", 2
    )(orb_rows, *tables)
    pieces, base_near = lax.optimization_barrier((pieces, to_near(message)))
    partners = pieces[:, ORB_DEV * PLANES :, :2].astype(jnp.int32).reshape(-1)
    served = call(
        serve_kernel,
        shape(devices, ENTRIES * PLANES, LANES),
        [SMEM, VMEM],
        [pltpu.VMEM((devices * ORB_DEV, PLANES, LANES), F32)],
        "serve",
        2,
    )(jnp.maximum(partners, 0), pieces)
    fetched = to_all(served)
    base_sums = from_pairs(base_ends, base_near)
    fetched, base_sums = lax.optimization_barrier((fetched, base_sums))
    total, base_energy = call(
        base_inverse_kernel,
        [totals, shape(ORB_DEV, LANES, dtype=F32)],
        [SMEM] + [VMEM] * (PAIRS + 5),
        [HELD] * ORB_DEV,
        "base_inverse",
        2,
    )(grid, base_near, *base_sums, base_coeffs, orb_rows, *tables)

    parts = []
    for start, count in PARTS:
        moved, coeffs, ends, message = call(
            functools.partial(pair_forward_kernel, start),
            [shape(count, ROWS, LANES)] + solve_shapes(count),
            [SMEM] * 2 + [VMEM] * 5,
            [SHIFT_BUFFER] * count + [HELD] * count,
            "pair_forward",
            2,
        )(pair_list, box_anchor, orb_rows, fetched, *tables)
        parts.append((start, moved, coeffs, ends, to_near(message)))
    start, moved, coeffs, ends, near = parts[0]
    total, near = lax.optimization_barrier((total, near))
    parts[0] = (start, moved, coeffs, ends, near)
    parts = [(*part, from_pairs(part[3], part[4], part[0] > 0)) for part in parts]
    back, energy = served, [base_energy]
    for start, moved, coeffs, ends, near, sums in parts:
        count = moved.shape[0]
        total, back, value = call(
            functools.partial(pair_inverse_kernel, start),
            [totals, shape(devices, (start + count) * PLANES, LANES), shape(count, LANES, dtype=F32)],
            [SMEM] * 3 + [VMEM] * (PAIRS + 7) + [VMEM if start else ANY],
            [SHIFT_BUFFER] * count + [HELD] * count,
            "pair_inverse",
            3,
            aliases={PAIRS + 9: 0},
        )(grid, pair_list, box_anchor, near, *sums, coeffs, orb_rows, moved, *tables, total, back)
        energy.append(value)

    arrived = to_all(back)
    energy = lax.psum(jnp.sum(jnp.concatenate(energy), axis=1), "grid")
    due, energy = call(
        gather_kernel,
        [shape(devices, spread, LANES), shape(ORB_DEV, LANES, dtype=F32)],
        [SMEM] * 2 + [VMEM, SMEM],
        [pltpu.VMEM((devices * ORB_DEV + 8, LANES), F32)]
        + [pltpu.VMEM((devices * ORB_DEV + 1, PLANES, LANES), F32)] * 4,
        "gather",
        4,
    )(jnp.where(partners >= 0, partners, devices * ORB_DEV), pair_list, arrived, energy)
    return call(
        finish_kernel,
        [shape(*orbitals.shape), shape(ORB_DEV, dtype=F32)],
        [VMEM] * 3,
        [],
        "finish",
        3,
        out_specs=[VMEM, SMEM],
    )(to_all(due), total, energy)


def solution(mesh):
    return jax.shard_map(
        local,
        mesh=mesh,
        in_specs=(P("orb", "grid", None), P(None, "orb"), P()),
        out_specs=(P("orb", "grid", None), P("orb")),
        check_vma=False,
    )
```
